32 devices in a mesh: seg: 4 (over y, x), pitch: 4 (over z), span: 2 (over core).
Axes of the slice: x: 2, y: 2, z: 4, core: 2. Of those that a mesh axis runs over, the one named last changes fastest.
Arguments:
- states: float32 [4, 5, 1024, 512], P('seg', None, 'pitch', 'span'), may hold values from -6 to 6
- forcing: float32 [4, 5, 1024, 512], P('seg', None, 'pitch', 'span'), may hold values from -6 to 6
- adv_pitch: float32 [5, 5], replicated, may hold values from -2.5 to 2.5
- adv_span: float32 [5, 5], replicated, may hold values from -2.5 to 2.5
- diffusion: float32 [5], replicated, may hold values from 0.1 to 0.4
Outputs:
- mismatch: float32 [4, 5, 1024, 512], P('seg', None, 'pitch', 'span')
- gradient: float32 [4, 5, 1024, 512], P('seg', None, 'pitch', 'span')
The draws below stay inside these ranges and needn't reach their ends.
All inputs are finite; a program needn't handle non-finite values.
Results may differ from the reference program's by a relative error of at most 0.0001.
Values sent between devices are 32-bit elements; how exact they have to be, the bound alone decides.
No kernel may reach another device: no remote copies, remote signals or barrier semaphores. Data moves between devices by JAX's collectives and lax.ppermute only.
A program may use at most 64 MiB of HBM per device.

```python
import math
import jax
import jax.numpy as jnp
from jax import lax

FIELDS = 5
SUBSTEPS = 2
SEGMENTS = 4
NP = 1024
NS = 512


def steps_of(key, extent, shards, low, top_value):
    level, own = 1.0, jax.random.fold_in(key, 6)
    for dim, parts in shards:
        heights = jnp.exp(jax.random.uniform(jax.random.fold_in(own, dim), (parts,), jnp.float32, low / len(shards), top_value / len(shards)))
        level = level * jnp.repeat(heights, extent[dim] // parts).reshape([-1 if axis == dim else 1 for axis in range(len(extent))])
    return level


def bell_draw(rng, shape, scale, bound, cuts=(), dtype=jnp.bfloat16):
    array = scale * jax.random.normal(rng, shape, jnp.float32)
    if cuts:
        array = array * steps_of(rng, shape, cuts, -0.22, 0.18)
    return jnp.clip(array, -bound, bound).astype(dtype)


def setup_inputs(seed: int = 0) -> dict:
    key_list = jax.random.split(jax.random.key(seed), 6)
    states = bell_draw(key_list[0], (SEGMENTS, FIELDS, NP, NS), 1.0, 6.0, ((0, 4), (2, 4), (3, 2)), jnp.float32)
    forcing = bell_draw(key_list[1], (SEGMENTS, FIELDS, NP, NS), 1.0, 6.0, ((0, 4), (2, 4), (3, 2)), jnp.float32)
    adv_pitch = bell_draw(key_list[2], (FIELDS, FIELDS), FIELDS ** -0.5, 2.5, (), jnp.float32)
    adv_span = bell_draw(key_list[3], (FIELDS, FIELDS), FIELDS ** -0.5, 2.5, (), jnp.float32)
    diffusion = jnp.clip(jnp.exp(jax.random.uniform(key_list[4], (FIELDS,), jnp.float32, math.log(0.1), math.log(0.4))), 0.1, 0.4)
    return {"states": states, "forcing": forcing, "adv_pitch": adv_pitch, "adv_span": adv_span, "diffusion": diffusion}


time_step = 0.25

def substep(field, mat_pitch, mat_span, viscous):
    padded = jnp.pad(field, ((0, 0), (1, 1), (0, 0)), mode='wrap')
    padded = jnp.pad(padded, ((0, 0), (0, 0), (1, 1)))
    centre = padded[:, 1:-1, 1:-1]
    along_pitch = (padded[:, 2:, 1:-1] - padded[:, :-2, 1:-1]) * 0.5
    along_span = (padded[:, 1:-1, 2:] - padded[:, 1:-1, :-2]) * 0.5
    laplace = padded[:, 2:, 1:-1] + padded[:, :-2, 1:-1] + padded[:, 1:-1, 2:] + padded[:, 1:-1, :-2] - 4.0 * centre
    flux = jnp.einsum('fg,gpq->fpq', mat_pitch, along_pitch, precision=lax.Precision.HIGHEST)
    flux = flux + jnp.einsum('fg,gpq->fpq', mat_span, along_span, precision=lax.Precision.HIGHEST)
    return centre + time_step * (flux + viscous[:, None, None] * laplace)

def reference(states, forcing, adv_pitch, adv_span, diffusion):

    def advance(field):
        for repeat in range(SUBSTEPS):
            field = substep(field, -adv_pitch, -adv_span, diffusion)
        return field
    ending = lax.map(advance, states) + time_step * forcing
    mismatch = ending - jnp.roll(states, -1, axis=0)

    def adjoint(residue):
        return jax.vjp(advance, jnp.zeros_like(residue))[1](residue)[0]
    gradient = lax.map(adjoint, mismatch) - jnp.roll(mismatch, 1, axis=0)
    return (mismatch, gradient)
```

```python
import functools

import jax
import jax.numpy as jnp
from jax import lax
from jax.experimental import pallas as pl
from jax.experimental.pallas import tpu as pltpu
from jax.sharding import PartitionSpec as P

TIME_STEP = 0.25
SUBSTEPS = 2
TILE = 8
LANES = 128
STRIP = 24
MARGIN = 2 * TILE
VMEM_LIMIT = 32 * 1024 * 1024


def edge_strip(field_of, fields, rows, cols):
    lane = lax.broadcasted_iota(jnp.int32, (rows, LANES), 1)
    packed = jnp.zeros((rows, LANES), jnp.float32)
    for f in range(fields):
        first, last = field_of(f, 0), field_of(f, cols - LANES)
        ends = jnp.where(lane < LANES // 2, first, last)
        moved = pltpu.roll(ends, 4 * f + 2, 1)
        packed = jnp.where((lane >= 4 * f) & (lane < 4 * f + 4), moved, packed)
    return jnp.transpose(packed)[:STRIP]


def edges_kernel(cells, strip):
    fields, rows, cols = cells.shape
    strip[...] = edge_strip(lambda f, at: cells[f, :, at : at + LANES], fields, rows, cols)


def mismatch_kernel(ending, following, mismatch, strip):
    fields, rows, cols = mismatch.shape
    for f in range(fields):
        mismatch[f] = ending[f] - following[f]
    strip[...] = edge_strip(lambda f, at: mismatch[f, :, at : at + LANES], fields, rows, cols)


def substep(source, tile, coefficients, width):
    pitch, span, near, keep = coefficients
    fields, _, lanes = source.shape
    window = pl.ds(pl.multiple_of((tile - 1) * TILE, TILE), 3 * TILE)
    along_pitch, along_span, around, centre = [], [], [], []
    for g in range(fields):
        rows = source.at[g, window]
        here = rows[TILE : 2 * TILE, :]
        below = rows[TILE + 1 : 2 * TILE + 1, :][:, :width]
        above = rows[TILE - 1 : 2 * TILE - 1, :][:, :width]
        right = pltpu.roll(here, lanes - 1, 1)[:, :width]
        left = pltpu.roll(here, 1, 1)[:, :width]
        along_pitch.append(below - above)
        along_span.append(right - left)
        around.append((below + above) + (right + left))
        centre.append(here[:, :width])
    results = []
    for f in range(fields):
        total = keep[f] * centre[f] + near[f] * around[f]
        for g in range(fields):
            total = total + pitch[f][g] * along_pitch[g]
            total = total + span[f][g] * along_span[g]
        results.append(total)
    return results


def propagate_kernel(
    transposed, sign, scale, position, mat_pitch, mat_span, viscous, cells, extra, strip, upper, lower, result, first, second
):
    fields, rows, cols = cells.shape
    lanes = cols + LANES
    has_left = position[0] > 0
    has_right = position[0] < position[1] - 1
    factor = sign * TIME_STEP * 0.5

    def entry(matrix, f, g):
        return factor * (matrix[g, f] if transposed else matrix[f, g])

    pitch = [[entry(mat_pitch, f, g) for g in range(fields)] for f in range(fields)]
    span = [[entry(mat_span, f, g) for g in range(fields)] for f in range(fields)]
    near = [TIME_STEP * viscous[f] for f in range(fields)]
    keep = [1.0 - 4.0 * TIME_STEP * viscous[f] for f in range(fields)]
    coefficients = (pitch, span, near, keep)

    def within(shape):
        side = lax.broadcasted_iota(jnp.int32, shape, 1) < LANES // 2
        return jnp.where(side, has_right.astype(jnp.int32), has_left.astype(jnp.int32)) > 0

    corner_above = jnp.concatenate([upper[f, :, cols:] for f in range(STRIP // TILE)], axis=0)
    corner_below = jnp.concatenate([lower[f, :, cols:] for f in range(STRIP // TILE)], axis=0)
    along = jnp.concatenate([corner_above, strip[...], corner_below], axis=1)
    along = jnp.concatenate([along, jnp.zeros((LANES - STRIP, along.shape[1]), jnp.float32)], axis=0)
    turned = jnp.transpose(along)[LANES - MARGIN : LANES + rows + MARGIN]
    inside = within(turned.shape)
    for f in range(fields):
        side = pltpu.roll(turned, LANES - (4 * f + 2), 1)
        first[f, :, cols:] = jnp.where(inside, side, 0.0)
        first[f, MARGIN - TILE : MARGIN, :cols] = upper[f, :, :cols]
        first[f, MARGIN + rows : MARGIN + rows + TILE, :cols] = lower[f, :, :cols]
        first[f, MARGIN : MARGIN + rows, :cols] = cells[f]

    inside_tile = within((TILE, LANES))

    def step_one(tile, carry):
        for f, value in enumerate(substep(first, tile, coefficients, lanes)):
            second[f, pl.ds(pl.multiple_of(tile * TILE, TILE), TILE), :cols] = value[:, :cols]
            second[f, pl.ds(pl.multiple_of(tile * TILE, TILE), TILE), cols:] = jnp.where(inside_tile, value[:, cols:], 0.0)
        return carry

    lax.fori_loop(1, (MARGIN + rows) // TILE + 1, step_one, 0)

    def step_two(tile, carry):
        for f, value in enumerate(substep(second, tile, coefficients, cols)):
            at = pl.ds(pl.multiple_of(tile * TILE - MARGIN, TILE), TILE)
            result[f, at, :] = value + scale * extra[f, at, :]
        return carry

    lax.fori_loop(MARGIN // TILE, (MARGIN + rows) // TILE, step_two, 0)


def finish_kernel(adjoint, arrived, gradient):
    gradient[...] = adjoint[...] - arrived[...]


def in_vmem(count):
    return [pl.BlockSpec(memory_space=pltpu.VMEM)] * count


def in_smem(count):
    return [pl.BlockSpec(memory_space=pltpu.SMEM)] * count


PARAMS = pltpu.CompilerParams(vmem_limit_bytes=VMEM_LIMIT)


def edges_of(cells):
    return pl.pallas_call(
        edges_kernel,
        out_shape=jax.ShapeDtypeStruct((STRIP, cells.shape[1]), jnp.float32),
        in_specs=in_vmem(1),
        out_specs=pl.BlockSpec(memory_space=pltpu.VMEM),
        compiler_params=PARAMS,
    )(cells)


def mismatch_of(ending, following):
    fields, rows, cols = ending.shape
    return pl.pallas_call(
        mismatch_kernel,
        out_shape=(
            jax.ShapeDtypeStruct(ending.shape, jnp.float32),
            jax.ShapeDtypeStruct((STRIP, rows), jnp.float32),
        ),
        in_specs=in_vmem(2),
        out_specs=tuple(in_vmem(2)),
        compiler_params=PARAMS,
    )(ending, following)


def exchanged(cells, strip):
    fields, rows, cols = cells.shape
    count = lax.axis_size("span")
    if count == 2:
        sides = lax.ppermute(strip, "span", [(0, 1), (1, 0)])
    else:
        from_left = lax.ppermute(strip, "span", [(i, i + 1) for i in range(count - 1)])
        from_right = lax.ppermute(strip, "span", [(i + 1, i) for i in range(count - 1)])
        kind = lax.broadcasted_iota(jnp.int32, strip.shape, 0) % 4
        sides = jnp.where(kind < 2, from_left, from_right)

    def outer(row, lane):
        ends = sides[:, lane : lane + LANES].reshape(STRIP // TILE, TILE, LANES)
        ends = jnp.pad(ends, ((0, fields - STRIP // TILE), (0, 0), (0, 0)))
        return jnp.concatenate([cells[:, row : row + TILE, :], ends], axis=2)

    ring = lax.axis_size("pitch")
    upper = lax.ppermute(outer(rows - TILE, rows - LANES), "pitch", [(i, (i + 1) % ring) for i in range(ring)])
    lower = lax.ppermute(outer(0, 0), "pitch", [((i + 1) % ring, i) for i in range(ring)])
    return sides, upper, lower


def propagated(position, mat_pitch, mat_span, viscous, cells, extra, halos, transposed, sign, scale):
    fields, rows, cols = cells.shape
    wide = pltpu.VMEM((fields, rows + 2 * MARGIN, cols + LANES), jnp.float32)
    return pl.pallas_call(
        functools.partial(propagate_kernel, transposed, sign, scale),
        out_shape=jax.ShapeDtypeStruct(cells.shape, jnp.float32),
        in_specs=in_smem(4) + in_vmem(5),
        out_specs=pl.BlockSpec(memory_space=pltpu.VMEM),
        scratch_shapes=[wide, wide],
        compiler_params=PARAMS,
    )(position, mat_pitch, mat_span, viscous, cells, extra, *halos)


def passed_along(shard, by):
    count = lax.axis_size("seg")
    return lax.ppermute(shard, "seg", [(i, (i + by) % count) for i in range(count)])


def body(states, forcing, adv_pitch, adv_span, diffusion):
    start = states[0]
    position = jnp.stack([lax.axis_index("span"), lax.axis_size("span")]).astype(jnp.int32)
    following = passed_along(start, -1)
    halos = exchanged(start, edges_of(start))
    ending = propagated(position, adv_pitch, adv_span, diffusion, start, forcing[0], halos, False, -1.0, TIME_STEP)
    arrived = passed_along(ending, 1)
    mismatch, strip = mismatch_of(ending, following)
    halos = exchanged(mismatch, strip)
    adjoint = propagated(position, adv_pitch, adv_span, diffusion, mismatch, start, halos, True, 1.0, 1.0)
    gradient = adjoint - arrived
    return (mismatch[None], gradient[None])


def solution(mesh):
    whole = P("seg", None, "pitch", "span")
    return jax.shard_map(
        body,
        mesh=mesh,
        in_specs=(whole, whole, P(), P(), P()),
        out_specs=(whole, whole),
        check_vma=False,
    )
```

```python
import functools

import jax
import jax.numpy as jnp
from jax import lax
from jax.experimental import pallas as pl
from jax.experimental.pallas import tpu as pltpu
from jax.sharding import PartitionSpec as P

TIME_STEP = 0.25
SUBSTEPS = 2
TILE = 8
LANES = 128
STRIP = 24
MARGIN = 2 * TILE
VMEM_LIMIT = 32 * 1024 * 1024


def edge_strip(field_of, fields, rows, cols):
    lane = lax.broadcasted_iota(jnp.int32, (rows, LANES), 1)
    packed = jnp.zeros((rows, LANES), jnp.float32)
    for f in range(fields):
        first, last = field_of(f, 0), field_of(f, cols - LANES)
        ends = jnp.where(lane < LANES // 2, first, last)
        moved = pltpu.roll(ends, 4 * f + 2, 1)
        packed = jnp.where((lane >= 4 * f) & (lane < 4 * f + 4), moved, packed)
    return jnp.transpose(packed)[:STRIP]


def edges_kernel(cells, strip):
    fields, rows, cols = cells.shape
    strip[...] = edge_strip(lambda f, at: cells[f, :, at : at + LANES], fields, rows, cols)


def mismatch_kernel(lead, last, following, mismatch, again, strip):
    fields, rows, cols = mismatch.shape
    for f in range(fields):
        ending = lead[f] if f < lead.shape[0] else last[f - lead.shape[0]]
        mismatch[f] = again[f] = ending - following[f]
    strip[...] = edge_strip(lambda f, at: mismatch[f, :, at : at + LANES], fields, rows, cols)


def substep(source, tile, coefficients, width):
    pitch, span, near, keep = coefficients
    fields, _, lanes = source.shape
    window = pl.ds(pl.multiple_of((tile - 1) * TILE, TILE), 3 * TILE)
    along_pitch, along_span, around, centre = [], [], [], []
    for g in range(fields):
        rows = source.at[g, window]
        here = rows[TILE : 2 * TILE, :]
        below = rows[TILE + 1 : 2 * TILE + 1, :][:, :width]
        above = rows[TILE - 1 : 2 * TILE - 1, :][:, :width]
        right = pltpu.roll(here, lanes - 1, 1)[:, :width]
        left = pltpu.roll(here, 1, 1)[:, :width]
        along_pitch.append(below - above)
        along_span.append(right - left)
        around.append((below + above) + (right + left))
        centre.append(here[:, :width])
    results = []
    for f in range(fields):
        total = keep[f] * centre[f] + near[f] * around[f]
        for g in range(fields):
            total = total + pitch[f][g] * along_pitch[g]
            total = total + span[f][g] * along_span[g]
        results.append(total)
    return results


def propagate_kernel(
    transposed, sign, scale, position, mat_pitch, mat_span, viscous, cells, extra, strip, upper, lower, lead, last, first, second
):
    fields, rows, cols = cells.shape
    lanes = cols + LANES
    has_left = position[0] > 0
    has_right = position[0] < position[1] - 1
    factor = sign * TIME_STEP * 0.5

    def entry(matrix, f, g):
        return factor * (matrix[g, f] if transposed else matrix[f, g])

    pitch = [[entry(mat_pitch, f, g) for g in range(fields)] for f in range(fields)]
    span = [[entry(mat_span, f, g) for g in range(fields)] for f in range(fields)]
    near = [TIME_STEP * viscous[f] for f in range(fields)]
    keep = [1.0 - 4.0 * TIME_STEP * viscous[f] for f in range(fields)]
    coefficients = (pitch, span, near, keep)

    def within(shape):
        side = lax.broadcasted_iota(jnp.int32, shape, 1) < LANES // 2
        return jnp.where(side, has_right.astype(jnp.int32), has_left.astype(jnp.int32)) > 0

    corner_above = jnp.concatenate([upper[f, :, cols:] for f in range(STRIP // TILE)], axis=0)
    corner_below = jnp.concatenate([lower[f, :, cols:] for f in range(STRIP // TILE)], axis=0)
    along = jnp.concatenate([corner_above, strip[...], corner_below], axis=1)
    along = jnp.concatenate([along, jnp.zeros((LANES - STRIP, along.shape[1]), jnp.float32)], axis=0)
    turned = jnp.transpose(along)[LANES - MARGIN : LANES + rows + MARGIN]
    inside = within(turned.shape)
    for f in range(fields):
        side = pltpu.roll(turned, LANES - (4 * f + 2), 1)
        first[f, :, cols:] = jnp.where(inside, side, 0.0)
        first[f, MARGIN - TILE : MARGIN, :cols] = upper[f, :, :cols]
        first[f, MARGIN + rows : MARGIN + rows + TILE, :cols] = lower[f, :, :cols]
        first[f, MARGIN : MARGIN + rows, :cols] = cells[f]

    inside_tile = within((TILE, LANES))

    def step_one(tile, carry):
        for f, value in enumerate(substep(first, tile, coefficients, lanes)):
            second[f, pl.ds(pl.multiple_of(tile * TILE, TILE), TILE), :cols] = value[:, :cols]
            second[f, pl.ds(pl.multiple_of(tile * TILE, TILE), TILE), cols:] = jnp.where(inside_tile, value[:, cols:], 0.0)
        return carry

    lax.fori_loop(1, (MARGIN + rows) // TILE + 1, step_one, 0)

    def step_two(tile, carry):
        for f, value in enumerate(substep(second, tile, coefficients, cols)):
            at = pl.ds(pl.multiple_of(tile * TILE - MARGIN, TILE), TILE)
            result, place = (lead, f) if f < lead.shape[0] else (last, f - lead.shape[0])
            result[place, at, :] = value + scale * extra[f, at, :]
        return carry

    lax.fori_loop(MARGIN // TILE, (MARGIN + rows) // TILE, step_two, 0)


def lead_kernel(adjoint, arrived, gradient):
    gradient[0] = adjoint[...] - arrived[...]


def last_kernel(adjoint, arrived, begun, gradient):
    gradient[0] = adjoint[...] - arrived[...]


def in_vmem(count):
    return [pl.BlockSpec(memory_space=pltpu.VMEM)] * count


def in_smem(count):
    return [pl.BlockSpec(memory_space=pltpu.SMEM)] * count


PARAMS = pltpu.CompilerParams(vmem_limit_bytes=VMEM_LIMIT)


def edges_of(cells):
    return pl.pallas_call(
        edges_kernel,
        out_shape=jax.ShapeDtypeStruct((STRIP, cells.shape[1]), jnp.float32),
        in_specs=in_vmem(1),
        out_specs=pl.BlockSpec(memory_space=pltpu.VMEM),
        compiler_params=PARAMS,
    )(cells)


def mismatch_of(lead, last, following):
    whole = jax.ShapeDtypeStruct(following.shape, jnp.float32)
    return pl.pallas_call(
        mismatch_kernel,
        out_shape=(whole, whole, jax.ShapeDtypeStruct((STRIP, following.shape[1]), jnp.float32)),
        in_specs=in_vmem(3),
        out_specs=tuple(in_vmem(3)),
        compiler_params=PARAMS,
    )(lead, last, following)


def gradient_of(adjoint, arrived):
    count, rows, cols = adjoint[0].shape
    rest = adjoint[1].shape[0]
    whole = jax.ShapeDtypeStruct((1, count + rest, rows, cols), jnp.float32)
    field = pl.BlockSpec((1, rows, cols), lambda f: (f, 0, 0))
    begun = pl.pallas_call(
        lead_kernel,
        grid=(count,),
        out_shape=whole,
        in_specs=[field, field],
        out_specs=pl.BlockSpec((1, 1, rows, cols), lambda f: (0, f, 0, 0)),
        compiler_params=PARAMS,
    )(adjoint[0], arrived[0])
    return pl.pallas_call(
        last_kernel,
        grid=(1,),
        out_shape=whole,
        in_specs=in_vmem(2) + [pl.BlockSpec(memory_space=pl.ANY)],
        out_specs=pl.BlockSpec((1, rest, rows, cols), lambda f: (0, count // rest, 0, 0)),
        input_output_aliases={2: 0},
        compiler_params=PARAMS,
    )(adjoint[1], arrived[1], begun)


def exchanged(cells, strip):
    fields, rows, cols = cells.shape
    count = lax.axis_size("span")
    if count == 2:
        sides = lax.ppermute(strip, "span", [(0, 1), (1, 0)])
    else:
        from_left = lax.ppermute(strip, "span", [(i, i + 1) for i in range(count - 1)])
        from_right = lax.ppermute(strip, "span", [(i + 1, i) for i in range(count - 1)])
        kind = lax.broadcasted_iota(jnp.int32, strip.shape, 0) % 4
        sides = jnp.where(kind < 2, from_left, from_right)

    def outer(row, lane):
        ends = sides[:, lane : lane + LANES].reshape(STRIP // TILE, TILE, LANES)
        ends = jnp.pad(ends, ((0, fields - STRIP // TILE), (0, 0), (0, 0)))
        return jnp.concatenate([cells[:, row : row + TILE, :], ends], axis=2)

    ring = lax.axis_size("pitch")
    upper = lax.ppermute(outer(rows - TILE, rows - LANES), "pitch", [(i, (i + 1) % ring) for i in range(ring)])
    lower = lax.ppermute(outer(0, 0), "pitch", [((i + 1) % ring, i) for i in range(ring)])
    return sides, upper, lower


def propagated(position, mat_pitch, mat_span, viscous, cells, extra, halos, transposed, sign, scale):
    fields, rows, cols = cells.shape
    wide = pltpu.VMEM((fields, rows + 2 * MARGIN, cols + LANES), jnp.float32)
    return pl.pallas_call(
        functools.partial(propagate_kernel, transposed, sign, scale),
        out_shape=tuple(jax.ShapeDtypeStruct((n, rows, cols), jnp.float32) for n in (fields - 1, 1)),
        in_specs=in_smem(4) + in_vmem(5),
        out_specs=tuple(in_vmem(2)),
        scratch_shapes=[wide, wide],
        compiler_params=PARAMS,
    )(position, mat_pitch, mat_span, viscous, cells, extra, *halos)


def passed_along(shard, by):
    count = lax.axis_size("seg")
    return lax.ppermute(shard, "seg", [(i, (i + by) % count) for i in range(count)])


def body(states, forcing, adv_pitch, adv_span, diffusion):
    start = states[0]
    position = jnp.stack([lax.axis_index("span"), lax.axis_size("span")]).astype(jnp.int32)
    following = passed_along(start, -1)
    halos = exchanged(start, edges_of(start))
    ending = propagated(position, adv_pitch, adv_span, diffusion, start, forcing[0], halos, False, -1.0, TIME_STEP)
    arrived = [passed_along(part, 1) for part in ending]
    mismatch, again, strip = mismatch_of(*ending, following)
    halos = exchanged(again, strip)
    adjoint = propagated(position, adv_pitch, adv_span, diffusion, again, start, halos, True, 1.0, 1.0)
    return (mismatch[None], gradient_of(adjoint, arrived))


def solution(mesh):
    whole = P("seg", None, "pitch", "span")
    return jax.shard_map(
        body,
        mesh=mesh,
        in_specs=(whole, whole, P(), P(), P()),
        out_specs=(whole, whole),
        check_vma=False,
    )
```

```python
import functools

import jax
import jax.numpy as jnp
from jax import lax
from jax.experimental import pallas as pl
from jax.experimental.pallas import tpu as pltpu
from jax.sharding import PartitionSpec as P

TIME_STEP = 0.25
SUBSTEPS = 2
TILE = 8
LANES = 128
STRIP = 24
MARGIN = 2 * TILE
LAST = 32
VMEM_LIMIT = 32 * 1024 * 1024


def edge_strip(field_of, fields, rows, cols):
    lane = lax.broadcasted_iota(jnp.int32, (rows, LANES), 1)
    packed = jnp.zeros((rows, LANES), jnp.float32)
    for f in range(fields):
        first, last = field_of(f, 0), field_of(f, cols - LANES)
        ends = jnp.where(lane < LANES // 2, first, last)
        moved = pltpu.roll(ends, 4 * f + 2, 1)
        packed = jnp.where((lane >= 4 * f) & (lane < 4 * f + 4), moved, packed)
    return jnp.transpose(packed)[:STRIP]


def edges_kernel(cells, strip):
    fields, rows, cols = cells.shape
    strip[...] = edge_strip(lambda f, at: cells[f, :, at : at + LANES], fields, rows, cols)


def mismatch_kernel(lead, last, following, mismatch, again, strip):
    fields, rows, cols = mismatch.shape
    begin = lead.shape[1]
    for f in range(fields):
        mismatch[f, :begin] = again[f, :begin] = lead[f] - following[f, :begin]
        mismatch[f, begin:] = again[f, begin:] = last[f] - following[f, begin:]
    strip[...] = edge_strip(lambda f, at: mismatch[f, :, at : at + LANES], fields, rows, cols)


def substep(source, tile, coefficients, width):
    pitch, span, near, keep = coefficients
    fields, _, lanes = source.shape
    window = pl.ds(pl.multiple_of((tile - 1) * TILE, TILE), 3 * TILE)
    along_pitch, along_span, around, centre = [], [], [], []
    for g in range(fields):
        rows = source.at[g, window]
        here = rows[TILE : 2 * TILE, :]
        below = rows[TILE + 1 : 2 * TILE + 1, :][:, :width]
        above = rows[TILE - 1 : 2 * TILE - 1, :][:, :width]
        right = pltpu.roll(here, lanes - 1, 1)[:, :width]
        left = pltpu.roll(here, 1, 1)[:, :width]
        along_pitch.append(below - above)
        along_span.append(right - left)
        around.append((below + above) + (right + left))
        centre.append(here[:, :width])
    results = []
    for f in range(fields):
        total = keep[f] * centre[f] + near[f] * around[f]
        for g in range(fields):
            total = total + pitch[f][g] * along_pitch[g]
            total = total + span[f][g] * along_span[g]
        results.append(total)
    return results


def propagate_kernel(
    transposed, sign, scale, position, mat_pitch, mat_span, viscous, cells, extra, strip, upper, lower, lead, last, first, second
):
    fields, rows, cols = cells.shape
    lanes = cols + LANES
    has_left = position[0] > 0
    has_right = position[0] < position[1] - 1
    factor = sign * TIME_STEP * 0.5

    def entry(matrix, f, g):
        return factor * (matrix[g, f] if transposed else matrix[f, g])

    pitch = [[entry(mat_pitch, f, g) for g in range(fields)] for f in range(fields)]
    span = [[entry(mat_span, f, g) for g in range(fields)] for f in range(fields)]
    near = [TIME_STEP * viscous[f] for f in range(fields)]
    keep = [1.0 - 4.0 * TIME_STEP * viscous[f] for f in range(fields)]
    coefficients = (pitch, span, near, keep)

    def within(shape):
        side = lax.broadcasted_iota(jnp.int32, shape, 1) < LANES // 2
        return jnp.where(side, has_right.astype(jnp.int32), has_left.astype(jnp.int32)) > 0

    corner_above = jnp.concatenate([upper[f, :, cols:] for f in range(STRIP // TILE)], axis=0)
    corner_below = jnp.concatenate([lower[f, :, cols:] for f in range(STRIP // TILE)], axis=0)
    along = jnp.concatenate([corner_above, strip[...], corner_below], axis=1)
    along = jnp.concatenate([along, jnp.zeros((LANES - STRIP, along.shape[1]), jnp.float32)], axis=0)
    turned = jnp.transpose(along)[LANES - MARGIN : LANES + rows + MARGIN]
    inside = within(turned.shape)
    for f in range(fields):
        side = pltpu.roll(turned, LANES - (4 * f + 2), 1)
        first[f, :, cols:] = jnp.where(inside, side, 0.0)
        first[f, MARGIN - TILE : MARGIN, :cols] = upper[f, :, :cols]
        first[f, MARGIN + rows : MARGIN + rows + TILE, :cols] = lower[f, :, :cols]
        first[f, MARGIN : MARGIN + rows, :cols] = cells[f]

    inside_tile = within((TILE, LANES))

    def step_one(tile, carry):
        for f, value in enumerate(substep(first, tile, coefficients, lanes)):
            second[f, pl.ds(pl.multiple_of(tile * TILE, TILE), TILE), :cols] = value[:, :cols]
            second[f, pl.ds(pl.multiple_of(tile * TILE, TILE), TILE), cols:] = jnp.where(inside_tile, value[:, cols:], 0.0)
        return carry

    lax.fori_loop(1, (MARGIN + rows) // TILE + 1, step_one, 0, unroll=2)

    def step_two(result, base, tile, carry):
        for f, value in enumerate(substep(second, tile, coefficients, cols)):
            at = pl.multiple_of(tile * TILE - MARGIN, TILE)
            into = pl.multiple_of(at - base, TILE)
            result[f, pl.ds(into, TILE), :] = value + scale * extra[f, pl.ds(at, TILE), :]
        return carry

    begin = lead.shape[1]
    bounds = [MARGIN // TILE, (MARGIN + begin) // TILE, (MARGIN + rows) // TILE]
    lax.fori_loop(bounds[0], bounds[1], functools.partial(step_two, lead, 0), 0, unroll=4)
    lax.fori_loop(bounds[1], bounds[2], functools.partial(step_two, last, begin), 0, unroll=4)


def lead_kernel(adjoint, arrived, gradient):
    gradient[0] = adjoint[...] - arrived[...]


def last_kernel(adjoint, early, late, begun, gradient):
    gradient[0] = adjoint[...] - (early[...] + late[...])


def in_vmem(count):
    return [pl.BlockSpec(memory_space=pltpu.VMEM)] * count


def in_smem(count):
    return [pl.BlockSpec(memory_space=pltpu.SMEM)] * count


PARAMS = pltpu.CompilerParams(vmem_limit_bytes=VMEM_LIMIT)


def edges_of(cells):
    return pl.pallas_call(
        edges_kernel,
        out_shape=jax.ShapeDtypeStruct((STRIP, cells.shape[1]), jnp.float32),
        in_specs=in_vmem(1),
        out_specs=pl.BlockSpec(memory_space=pltpu.VMEM),
        compiler_params=PARAMS,
    )(cells)


def mismatch_of(lead, last, following):
    whole = jax.ShapeDtypeStruct(following.shape, jnp.float32)
    return pl.pallas_call(
        mismatch_kernel,
        out_shape=(whole, whole, jax.ShapeDtypeStruct((STRIP, following.shape[1]), jnp.float32)),
        in_specs=in_vmem(3),
        out_specs=tuple(in_vmem(3)),
        compiler_params=PARAMS,
    )(lead, last, following)


def gradient_of(adjoint, arrived):
    fields, begin, cols = adjoint[0].shape
    rest = adjoint[1].shape[1]
    whole = jax.ShapeDtypeStruct((1, fields, begin + rest, cols), jnp.float32)
    begun = pl.pallas_call(
        lead_kernel,
        grid=(1,),
        out_shape=whole,
        in_specs=in_vmem(2),
        out_specs=pl.BlockSpec((1, fields, begin, cols), lambda i: (0, 0, 0, 0)),
        compiler_params=PARAMS,
    )(adjoint[0], arrived[0])
    return pl.pallas_call(
        last_kernel,
        grid=(1,),
        out_shape=whole,
        in_specs=in_vmem(3) + [pl.BlockSpec(memory_space=pl.ANY)],
        out_specs=pl.BlockSpec((1, fields, rest, cols), lambda f: (0, 0, begin // rest, 0)),
        input_output_aliases={3: 0},
        compiler_params=PARAMS,
    )(adjoint[1], *arrived[1], begun)


def exchanged(cells, strip):
    fields, rows, cols = cells.shape
    count = lax.axis_size("span")
    if count == 2:
        sides = lax.ppermute(strip, "span", [(0, 1), (1, 0)])
    else:
        from_left = lax.ppermute(strip, "span", [(i, i + 1) for i in range(count - 1)])
        from_right = lax.ppermute(strip, "span", [(i + 1, i) for i in range(count - 1)])
        kind = lax.broadcasted_iota(jnp.int32, strip.shape, 0) % 4
        sides = jnp.where(kind < 2, from_left, from_right)

    def outer(row, lane):
        ends = sides[:, lane : lane + LANES].reshape(STRIP // TILE, TILE, LANES)
        ends = jnp.pad(ends, ((0, fields - STRIP // TILE), (0, 0), (0, 0)))
        return jnp.concatenate([cells[:, row : row + TILE, :], ends], axis=2)

    ring = lax.axis_size("pitch")
    upper = lax.ppermute(outer(rows - TILE, rows - LANES), "pitch", [(i, (i + 1) % ring) for i in range(ring)])
    lower = lax.ppermute(outer(0, 0), "pitch", [((i + 1) % ring, i) for i in range(ring)])
    return sides, upper, lower


def propagated(position, mat_pitch, mat_span, viscous, cells, extra, halos, transposed, sign, scale):
    fields, rows, cols = cells.shape
    wide = pltpu.VMEM((fields, rows + 2 * MARGIN, cols + LANES), jnp.float32)
    return pl.pallas_call(
        functools.partial(propagate_kernel, transposed, sign, scale),
        out_shape=tuple(jax.ShapeDtypeStruct((fields, n, cols), jnp.float32) for n in (rows - LAST, LAST)),
        in_specs=in_smem(4) + in_vmem(5),
        out_specs=tuple(in_vmem(2)),
        scratch_shapes=[wide, wide],
        compiler_params=PARAMS,
    )(position, mat_pitch, mat_span, viscous, cells, extra, *halos)


def passed_along(shard, by):
    count = lax.axis_size("seg")
    return lax.ppermute(shard, "seg", [(i, (i + by) % count) for i in range(count)])


def passed_in_turn(shard, after, by):
    count, width = lax.axis_size("seg"), lax.axis_size("span")

    def share(cells, parity):
        pairs = [(i * width + k, (i + by) % count * width + k) for i in range(count) for k in range(parity, width, 2)]
        return lax.ppermute(cells, ("seg", "span"), pairs)

    early = share(shard, 0)
    late = share(lax.optimization_barrier((shard, after))[0], 1)
    return early, late


def body(states, forcing, adv_pitch, adv_span, diffusion):
    start = states[0]
    position = jnp.stack([lax.axis_index("span"), lax.axis_size("span")]).astype(jnp.int32)
    following = passed_along(start, -1)
    halos = exchanged(start, edges_of(start))
    ending = propagated(position, adv_pitch, adv_span, diffusion, start, forcing[0], halos, False, -1.0, TIME_STEP)
    arrived = [passed_along(ending[0], 1)]
    mismatch, again, strip = mismatch_of(*ending, following)
    halos = exchanged(again, strip)
    adjoint = propagated(position, adv_pitch, adv_span, diffusion, again, start, halos, True, 1.0, 1.0)
    arrived.append(passed_in_turn(ending[1], adjoint[0], 1))
    return (mismatch[None], gradient_of(adjoint, arrived))


def solution(mesh):
    whole = P("seg", None, "pitch", "span")
    return jax.shard_map(
        body,
        mesh=mesh,
        in_specs=(whole, whole, P(), P(), P()),
        out_specs=(whole, whole),
        check_vma=False,
    )
```

```python
import functools

import jax
import jax.numpy as jnp
from jax import lax
from jax.experimental import pallas as pl
from jax.experimental.pallas import tpu as pltpu
from jax.sharding import PartitionSpec as P

TIME_STEP = 0.25
SUBSTEPS = 2
TILE = 8
LANES = 128
STRIP = 24
MARGIN = 2 * TILE
LAST = 32
VMEM_LIMIT = 32 * 1024 * 1024


def edge_strip(field_of, fields, rows, cols):
    lane = lax.broadcasted_iota(jnp.int32, (rows, LANES), 1)
    packed = jnp.zeros((rows, LANES), jnp.float32)
    for f in range(fields):
        first, last = field_of(f, 0), field_of(f, cols - LANES)
        ends = jnp.where(lane < LANES // 2, first, last)
        moved = pltpu.roll(ends, 4 * f + 2, 1)
        packed = jnp.where((lane >= 4 * f) & (lane < 4 * f + 4), moved, packed)
    return jnp.transpose(packed)[:STRIP]


def edges_kernel(cells, strip):
    fields, rows, cols = cells.shape
    strip[...] = edge_strip(lambda f, at: cells[f, :, at : at + LANES], fields, rows, cols)


def mismatch_kernel(lead, last, following, mismatch, again, strip):
    fields, rows, cols = mismatch.shape
    begin = lead.shape[1]
    for f in range(fields):
        mismatch[f, :begin] = again[f, :begin] = lead[f] - following[f, :begin]
        mismatch[f, begin:] = again[f, begin:] = last[f] - following[f, begin:]
    strip[...] = edge_strip(lambda f, at: mismatch[f, :, at : at + LANES], fields, rows, cols)


def substep(source, tile, coefficients, width):
    pitch, span, near, keep = coefficients
    fields, _, lanes = source.shape
    window = pl.ds(pl.multiple_of((tile - 1) * TILE, TILE), 3 * TILE)
    along_pitch, along_span, around, centre = [], [], [], []
    for g in range(fields):
        rows = source.at[g, window]
        here = rows[TILE : 2 * TILE, :]
        below = rows[TILE + 1 : 2 * TILE + 1, :][:, :width]
        above = rows[TILE - 1 : 2 * TILE - 1, :][:, :width]
        right = pltpu.roll(here, lanes - 1, 1)[:, :width]
        left = pltpu.roll(here, 1, 1)[:, :width]
        along_pitch.append(below - above)
        along_span.append(right - left)
        around.append((below + above) + (right + left))
        centre.append(here[:, :width])
    results = []
    for f in range(fields):
        total = keep[f] * centre[f] + near[f] * around[f]
        for g in range(fields):
            total = total + pitch[f][g] * along_pitch[g]
            total = total + span[f][g] * along_span[g]
        results.append(total)
    return results


def propagate_kernel(
    transposed, sign, scale, position, mat_pitch, mat_span, viscous, cells, extra, strip, upper, lower, lead, last, first, second
):
    fields, rows, cols = cells.shape
    lanes = cols + LANES
    has_left = position[0] > 0
    has_right = position[0] < position[1] - 1
    factor = sign * TIME_STEP * 0.5

    def entry(matrix, f, g):
        return factor * (matrix[g, f] if transposed else matrix[f, g])

    pitch = [[entry(mat_pitch, f, g) for g in range(fields)] for f in range(fields)]
    span = [[entry(mat_span, f, g) for g in range(fields)] for f in range(fields)]
    near = [TIME_STEP * viscous[f] for f in range(fields)]
    keep = [1.0 - 4.0 * TIME_STEP * viscous[f] for f in range(fields)]
    coefficients = (pitch, span, near, keep)

    def within(shape):
        side = lax.broadcasted_iota(jnp.int32, shape, 1) < LANES // 2
        return jnp.where(side, has_right.astype(jnp.int32), has_left.astype(jnp.int32)) > 0

    corner_above = jnp.concatenate([upper[f, :, cols:] for f in range(STRIP // TILE)], axis=0)
    corner_below = jnp.concatenate([lower[f, :, cols:] for f in range(STRIP // TILE)], axis=0)
    along = jnp.concatenate([corner_above, strip[...], corner_below], axis=1)
    along = jnp.concatenate([along, jnp.zeros((LANES - STRIP, along.shape[1]), jnp.float32)], axis=0)
    turned = jnp.transpose(along)[LANES - MARGIN : LANES + rows + MARGIN]
    inside = within(turned.shape)
    for f in range(fields):
        side = pltpu.roll(turned, LANES - (4 * f + 2), 1)
        first[f, :, cols:] = jnp.where(inside, side, 0.0)
        first[f, MARGIN - TILE : MARGIN, :cols] = upper[f, :, :cols]
        first[f, MARGIN + rows : MARGIN + rows + TILE, :cols] = lower[f, :, :cols]
        first[f, MARGIN : MARGIN + rows, :cols] = cells[f]

    inside_tile = within((TILE, LANES))

    def step_one(tile, carry):
        for f, value in enumerate(substep(first, tile, coefficients, lanes)):
            second[f, pl.ds(pl.multiple_of(tile * TILE, TILE), TILE), :cols] = value[:, :cols]
            second[f, pl.ds(pl.multiple_of(tile * TILE, TILE), TILE), cols:] = jnp.where(inside_tile, value[:, cols:], 0.0)
        return carry

    lax.fori_loop(1, (MARGIN + rows) // TILE + 1, step_one, 0, unroll=2)

    def step_two(result, base, tile, carry):
        for f, value in enumerate(substep(second, tile, coefficients, cols)):
            at = pl.multiple_of(tile * TILE - MARGIN, TILE)
            into = pl.multiple_of(at - base, TILE)
            result[f, pl.ds(into, TILE), :] = value + scale * extra[f, pl.ds(at, TILE), :]
        return carry

    begin = lead.shape[1]
    bounds = [MARGIN // TILE, (MARGIN + begin) // TILE, (MARGIN + rows) // TILE]
    lax.fori_loop(bounds[0], bounds[1], functools.partial(step_two, lead, 0), 0, unroll=4)
    lax.fori_loop(bounds[1], bounds[2], functools.partial(step_two, last, begin), 0, unroll=4)


def lead_kernel(adjoint, arrived, gradient):
    gradient[0] = adjoint[...] - arrived[...]


def last_kernel(adjoint, arrived, begun, gradient):
    gradient[0] = adjoint[...] - arrived[...]


def in_vmem(count):
    return [pl.BlockSpec(memory_space=pltpu.VMEM)] * count


def in_smem(count):
    return [pl.BlockSpec(memory_space=pltpu.SMEM)] * count


PARAMS = pltpu.CompilerParams(vmem_limit_bytes=VMEM_LIMIT)


def edges_of(cells):
    return pl.pallas_call(
        edges_kernel,
        out_shape=jax.ShapeDtypeStruct((STRIP, cells.shape[1]), jnp.float32),
        in_specs=in_vmem(1),
        out_specs=pl.BlockSpec(memory_space=pltpu.VMEM),
        compiler_params=PARAMS,
    )(cells)


def mismatch_of(lead, last, following):
    whole = jax.ShapeDtypeStruct(following.shape, jnp.float32)
    return pl.pallas_call(
        mismatch_kernel,
        out_shape=(whole, whole, jax.ShapeDtypeStruct((STRIP, following.shape[1]), jnp.float32)),
        in_specs=in_vmem(3),
        out_specs=tuple(in_vmem(3)),
        compiler_params=PARAMS,
    )(lead, last, following)


def gradient_of(adjoint, arrived):
    fields, begin, cols = adjoint[0].shape
    rest = adjoint[1].shape[1]
    whole = jax.ShapeDtypeStruct((1, fields, begin + rest, cols), jnp.float32)
    begun = pl.pallas_call(
        lead_kernel,
        grid=(1,),
        out_shape=whole,
        in_specs=in_vmem(2),
        out_specs=pl.BlockSpec((1, fields, begin, cols), lambda i: (0, 0, 0, 0)),
        compiler_params=PARAMS,
    )(adjoint[0], arrived[0])
    return pl.pallas_call(
        last_kernel,
        grid=(1,),
        out_shape=whole,
        in_specs=in_vmem(2) + [pl.BlockSpec(memory_space=pl.ANY)],
        out_specs=pl.BlockSpec((1, fields, rest, cols), lambda f: (0, 0, begin // rest, 0)),
        input_output_aliases={2: 0},
        compiler_params=PARAMS,
    )(adjoint[1], arrived[1], begun)


def exchanged(cells, strip):
    fields, rows, cols = cells.shape
    count = lax.axis_size("span")
    if count == 2:
        sides = lax.ppermute(strip, "span", [(0, 1), (1, 0)])
    else:
        from_left = lax.ppermute(strip, "span", [(i, i + 1) for i in range(count - 1)])
        from_right = lax.ppermute(strip, "span", [(i + 1, i) for i in range(count - 1)])
        kind = lax.broadcasted_iota(jnp.int32, strip.shape, 0) % 4
        sides = jnp.where(kind < 2, from_left, from_right)

    def outer(row, lane):
        ends = sides[:, lane : lane + LANES].reshape(STRIP // TILE, TILE, LANES)
        ends = jnp.pad(ends, ((0, fields - STRIP // TILE), (0, 0), (0, 0)))
        return jnp.concatenate([cells[:, row : row + TILE, :], ends], axis=2)

    ring = lax.axis_size("pitch")
    upper = lax.ppermute(outer(rows - TILE, rows - LANES), "pitch", [(i, (i + 1) % ring) for i in range(ring)])
    lower = lax.ppermute(outer(0, 0), "pitch", [((i + 1) % ring, i) for i in range(ring)])
    return sides, upper, lower


def propagated(position, mat_pitch, mat_span, viscous, cells, extra, halos, transposed, sign, scale):
    fields, rows, cols = cells.shape
    wide = pltpu.VMEM((fields, rows + 2 * MARGIN, cols + LANES), jnp.float32)
    return pl.pallas_call(
        functools.partial(propagate_kernel, transposed, sign, scale),
        out_shape=tuple(jax.ShapeDtypeStruct((fields, n, cols), jnp.float32) for n in (rows - LAST, LAST)),
        in_specs=in_smem(4) + in_vmem(5),
        out_specs=tuple(in_vmem(2)),
        scratch_shapes=[wide, wide],
        compiler_params=PARAMS,
    )(position, mat_pitch, mat_span, viscous, cells, extra, *halos)


def passed_along(shard, by):
    count = lax.axis_size("seg")
    return lax.ppermute(shard, "seg", [(i, (i + by) % count) for i in range(count)])


def passed_by_swap(shard):
    count = lax.axis_size("seg")
    if count % 2:
        return passed_along(shard, 1)
    held = lax.ppermute(shard, "seg", [(i, (i + 2) % count if i % 2 else i) for i in range(count)])
    return lax.ppermute(held, "seg", [(i, i ^ 1) for i in range(count)])


def body(states, forcing, adv_pitch, adv_span, diffusion):
    start = states[0]
    position = jnp.stack([lax.axis_index("span"), lax.axis_size("span")]).astype(jnp.int32)
    following = passed_along(start, -1)
    halos = exchanged(start, edges_of(start))
    ending = propagated(position, adv_pitch, adv_span, diffusion, start, forcing[0], halos, False, -1.0, TIME_STEP)
    arrived = [passed_along(ending[0], 1), passed_by_swap(ending[1])]
    mismatch, again, strip = mismatch_of(*ending, following)
    halos = exchanged(again, strip)
    adjoint = propagated(position, adv_pitch, adv_span, diffusion, again, start, halos, True, 1.0, 1.0)
    return (mismatch[None], gradient_of(adjoint, arrived))


def solution(mesh):
    whole = P("seg", None, "pitch", "span")
    return jax.shard_map(
        body,
        mesh=mesh,
        in_specs=(whole, whole, P(), P(), P()),
        out_specs=(whole, whole),
        check_vma=False,
    )
```

```python
import functools

import jax
import jax.numpy as jnp
from jax import lax
from jax.experimental import pallas as pl
from jax.experimental.pallas import tpu as pltpu
from jax.sharding import PartitionSpec as P

TIME_STEP = 0.25
SUBSTEPS = 2
TILE = 8
LANES = 128
STRIP = 24
MARGIN = 2 * TILE
LAST = 32
VMEM_LIMIT = 32 * 1024 * 1024


def edge_strip(field_of, fields, rows, cols):
    lane = lax.broadcasted_iota(jnp.int32, (rows, LANES), 1)
    packed = jnp.zeros((rows, LANES), jnp.float32)
    for f in range(fields):
        first, last = field_of(f, 0), field_of(f, cols - LANES)
        ends = jnp.where(lane < LANES // 2, first, last)
        moved = pltpu.roll(ends, 4 * f + 2, 1)
        packed = jnp.where((lane >= 4 * f) & (lane < 4 * f + 4), moved, packed)
    return jnp.transpose(packed)[:STRIP]


def edges_kernel(cells, strip):
    fields, rows, cols = cells.shape
    strip[...] = edge_strip(lambda f, at: cells[f, :, at : at + LANES], fields, rows, cols)


def mismatch_kernel(lead, last, following, mismatch, again, strip):
    fields, rows, cols = mismatch.shape
    begin = lead.shape[1]
    for f in range(fields):
        mismatch[f, :begin] = again[f, :begin] = lead[f] - following[f, :begin]
        mismatch[f, begin:] = again[f, begin:] = last[f] - following[f, begin:]
    strip[...] = edge_strip(lambda f, at: mismatch[f, :, at : at + LANES], fields, rows, cols)


def substep(source, tile, coefficients, width):
    pitch, span, near, keep = coefficients
    fields, _, lanes = source.shape
    window = pl.ds(pl.multiple_of((tile - 1) * TILE, TILE), 3 * TILE)
    along_pitch, along_span, around, centre = [], [], [], []
    for g in range(fields):
        rows = source.at[g, window]
        here = rows[TILE : 2 * TILE, :]
        below = rows[TILE + 1 : 2 * TILE + 1, :][:, :width]
        above = rows[TILE - 1 : 2 * TILE - 1, :][:, :width]
        right = pltpu.roll(here, lanes - 1, 1)[:, :width]
        left = pltpu.roll(here, 1, 1)[:, :width]
        along_pitch.append(below - above)
        along_span.append(right - left)
        around.append((below + above) + (right + left))
        centre.append(here[:, :width])
    results = []
    for f in range(fields):
        total = keep[f] * centre[f] + near[f] * around[f]
        for g in range(fields):
            total = total + pitch[f][g] * along_pitch[g]
            total = total + span[f][g] * along_span[g]
        results.append(total)
    return results


def propagate_kernel(
    transposed, sign, scale, position, mat_pitch, mat_span, viscous, cells, extra, strip, upper, lower, lead, last, first, second
):
    fields, rows, cols = cells.shape
    lanes = cols + LANES
    has_left = position[0] > 0
    has_right = position[0] < position[1] - 1
    factor = sign * TIME_STEP * 0.5

    def entry(matrix, f, g):
        return factor * (matrix[g, f] if transposed else matrix[f, g])

    pitch = [[entry(mat_pitch, f, g) for g in range(fields)] for f in range(fields)]
    span = [[entry(mat_span, f, g) for g in range(fields)] for f in range(fields)]
    near = [TIME_STEP * viscous[f] for f in range(fields)]
    keep = [1.0 - 4.0 * TIME_STEP * viscous[f] for f in range(fields)]
    coefficients = (pitch, span, near, keep)

    def within(shape):
        side = lax.broadcasted_iota(jnp.int32, shape, 1) < LANES // 2
        return jnp.where(side, has_right.astype(jnp.int32), has_left.astype(jnp.int32)) > 0

    corner_above = jnp.concatenate([upper[f, :, cols:] for f in range(STRIP // TILE)], axis=0)
    corner_below = jnp.concatenate([lower[f, :, cols:] for f in range(STRIP // TILE)], axis=0)
    along = jnp.concatenate([corner_above, strip[...], corner_below], axis=1)
    along = jnp.concatenate([along, jnp.zeros((LANES - STRIP, along.shape[1]), jnp.float32)], axis=0)
    turned = jnp.transpose(along)[LANES - MARGIN : LANES + rows + MARGIN]
    inside = within(turned.shape)
    for f in range(fields):
        side = pltpu.roll(turned, LANES - (4 * f + 2), 1)
        first[f, :, cols:] = jnp.where(inside, side, 0.0)
        first[f, MARGIN - TILE : MARGIN, :cols] = upper[f, :, :cols]
        first[f, MARGIN + rows : MARGIN + rows + TILE, :cols] = lower[f, :, :cols]
        first[f, MARGIN : MARGIN + rows, :cols] = cells[f]

    inside_tile = within((TILE, LANES))

    def step_one(tile, carry):
        for f, value in enumerate(substep(first, tile, coefficients, lanes)):
            second[f, pl.ds(pl.multiple_of(tile * TILE, TILE), TILE), :cols] = value[:, :cols]
            second[f, pl.ds(pl.multiple_of(tile * TILE, TILE), TILE), cols:] = jnp.where(inside_tile, value[:, cols:], 0.0)
        return carry

    lax.fori_loop(1, (MARGIN + rows) // TILE + 1, step_one, 0, unroll=2)

    def step_two(result, base, tile, carry):
        for f, value in enumerate(substep(second, tile, coefficients, cols)):
            at = pl.multiple_of(tile * TILE - MARGIN, TILE)
            into = pl.multiple_of(at - base, TILE)
            result[f, pl.ds(into, TILE), :] = value + scale * extra[f, pl.ds(at, TILE), :]
        return carry

    begin = lead.shape[1]
    bounds = [MARGIN // TILE, (MARGIN + begin) // TILE, (MARGIN + rows) // TILE]
    lax.fori_loop(bounds[0], bounds[1], functools.partial(step_two, lead, 0), 0, unroll=4)
    lax.fori_loop(bounds[1], bounds[2], functools.partial(step_two, last, begin), 0, unroll=4)


def lead_kernel(adjoint, arrived, gradient):
    gradient[0] = adjoint[...] - arrived[...]


def last_kernel(adjoint, early, late, begun, gradient):
    gradient[0] = adjoint[...] - (early[...] + late[...])


def in_vmem(count):
    return [pl.BlockSpec(memory_space=pltpu.VMEM)] * count


def in_smem(count):
    return [pl.BlockSpec(memory_space=pltpu.SMEM)] * count


PARAMS = pltpu.CompilerParams(vmem_limit_bytes=VMEM_LIMIT)


def edges_of(cells):
    return pl.pallas_call(
        edges_kernel,
        out_shape=jax.ShapeDtypeStruct((STRIP, cells.shape[1]), jnp.float32),
        in_specs=in_vmem(1),
        out_specs=pl.BlockSpec(memory_space=pltpu.VMEM),
        compiler_params=PARAMS,
    )(cells)


def mismatch_of(lead, last, following):
    whole = jax.ShapeDtypeStruct(following.shape, jnp.float32)
    return pl.pallas_call(
        mismatch_kernel,
        out_shape=(whole, whole, jax.ShapeDtypeStruct((STRIP, following.shape[1]), jnp.float32)),
        in_specs=in_vmem(3),
        out_specs=tuple(in_vmem(3)),
        compiler_params=PARAMS,
    )(lead, last, following)


def gradient_of(adjoint, arrived):
    fields, begin, cols = adjoint[0].shape
    rest = adjoint[1].shape[1]
    whole = jax.ShapeDtypeStruct((1, fields, begin + rest, cols), jnp.float32)
    begun = pl.pallas_call(
        lead_kernel,
        grid=(1,),
        out_shape=whole,
        in_specs=in_vmem(2),
        out_specs=pl.BlockSpec((1, fields, begin, cols), lambda i: (0, 0, 0, 0)),
        compiler_params=PARAMS,
    )(adjoint[0], arrived[0])
    return pl.pallas_call(
        last_kernel,
        grid=(1,),
        out_shape=whole,
        in_specs=in_vmem(3) + [pl.BlockSpec(memory_space=pl.ANY)],
        out_specs=pl.BlockSpec((1, fields, rest, cols), lambda f: (0, 0, begin // rest, 0)),
        input_output_aliases={3: 0},
        compiler_params=PARAMS,
    )(adjoint[1], *arrived[1], begun)


def exchanged(cells, strip):
    fields, rows, cols = cells.shape
    count = lax.axis_size("span")
    if count == 2:
        sides = lax.ppermute(strip, "span", [(0, 1), (1, 0)])
    else:
        from_left = lax.ppermute(strip, "span", [(i, i + 1) for i in range(count - 1)])
        from_right = lax.ppermute(strip, "span", [(i + 1, i) for i in range(count - 1)])
        kind = lax.broadcasted_iota(jnp.int32, strip.shape, 0) % 4
        sides = jnp.where(kind < 2, from_left, from_right)

    def outer(row, lane):
        ends = sides[:, lane : lane + LANES].reshape(STRIP // TILE, TILE, LANES)
        ends = jnp.pad(ends, ((0, fields - STRIP // TILE), (0, 0), (0, 0)))
        return jnp.concatenate([cells[:, row : row + TILE, :], ends], axis=2)

    ring = lax.axis_size("pitch")
    upper = lax.ppermute(outer(rows - TILE, rows - LANES), "pitch", [(i, (i + 1) % ring) for i in range(ring)])
    lower = lax.ppermute(outer(0, 0), "pitch", [((i + 1) % ring, i) for i in range(ring)])
    return sides, upper, lower


def propagated(position, mat_pitch, mat_span, viscous, cells, extra, halos, transposed, sign, scale):
    fields, rows, cols = cells.shape
    wide = pltpu.VMEM((fields, rows + 2 * MARGIN, cols + LANES), jnp.float32)
    return pl.pallas_call(
        functools.partial(propagate_kernel, transposed, sign, scale),
        out_shape=tuple(jax.ShapeDtypeStruct((fields, n, cols), jnp.float32) for n in (rows - LAST, LAST)),
        in_specs=in_smem(4) + in_vmem(5),
        out_specs=tuple(in_vmem(2)),
        scratch_shapes=[wide, wide],
        compiler_params=PARAMS,
    )(position, mat_pitch, mat_span, viscous, cells, extra, *halos)


def passed_along(shard, by):
    count = lax.axis_size("seg")
    return lax.ppermute(shard, "seg", [(i, (i + by) % count) for i in range(count)])


def passed_by_swap(shard, after):
    count, width = lax.axis_size("seg"), lax.axis_size("span")
    held = lax.ppermute(shard, "seg", [(i, (i + 2) % count if i % 2 else i) for i in range(count)])

    def swapped(cells, parity):
        pairs = [(i * width + k, (i ^ 1) * width + k) for i in range(count) for k in range(parity, width, 2)]
        return lax.ppermute(cells, ("seg", "span"), pairs)

    early = swapped(held, 0)
    late = swapped(lax.optimization_barrier((held, after))[0], 1)
    return early, late


def body(states, forcing, adv_pitch, adv_span, diffusion):
    start = states[0]
    position = jnp.stack([lax.axis_index("span"), lax.axis_size("span")]).astype(jnp.int32)
    following = passed_along(start, -1)
    halos = exchanged(start, edges_of(start))
    ending = propagated(position, adv_pitch, adv_span, diffusion, start, forcing[0], halos, False, -1.0, TIME_STEP)
    arrived = [passed_along(ending[0], 1)]
    mismatch, again, strip = mismatch_of(*ending, following)
    halos = exchanged(again, strip)
    adjoint = propagated(position, adv_pitch, adv_span, diffusion, again, start, halos, True, 1.0, 1.0)
    arrived.append(passed_by_swap(ending[1], adjoint[0]))
    return (mismatch[None], gradient_of(adjoint, arrived))


def solution(mesh):
    whole = P("seg", None, "pitch", "span")
    return jax.shard_map(
        body,
        mesh=mesh,
        in_specs=(whole, whole, P(), P(), P()),
        out_specs=(whole, whole),
        check_vma=False,
    )
```

```python
import functools

import jax
import jax.numpy as jnp
from jax import lax
from jax.experimental import pallas as pl
from jax.experimental.pallas import tpu as pltpu
from jax.sharding import PartitionSpec as P

TIME_STEP = 0.25
SUBSTEPS = 2
TILE = 8
LANES = 128
STRIP = 24
MARGIN = 2 * TILE
LAST = 32
VMEM_LIMIT = 32 * 1024 * 1024


def edge_strip(field_of, fields, rows, cols):
    lane = lax.broadcasted_iota(jnp.int32, (rows, LANES), 1)
    packed = jnp.zeros((rows, LANES), jnp.float32)
    for f in range(fields):
        first, last = field_of(f, 0), field_of(f, cols - LANES)
        ends = jnp.where(lane < LANES // 2, first, last)
        moved = pltpu.roll(ends, 4 * f + 2, 1)
        packed = jnp.where((lane >= 4 * f) & (lane < 4 * f + 4), moved, packed)
    return jnp.transpose(packed)[:STRIP]


def edges_kernel(cells, strip):
    fields, rows, cols = cells.shape
    strip[...] = edge_strip(lambda f, at: cells[f, :, at : at + LANES], fields, rows, cols)


def mismatch_kernel(lead, last, following, mismatch, again, strip):
    fields, rows, cols = mismatch.shape
    begin = lead.shape[1]
    for f in range(fields):
        mismatch[f, :begin] = again[f, :begin] = lead[f] - following[f, :begin]
        mismatch[f, begin:] = again[f, begin:] = last[f] - following[f, begin:]
    strip[...] = edge_strip(lambda f, at: mismatch[f, :, at : at + LANES], fields, rows, cols)


def substep(source, tile, coefficients, width):
    pitch, span, near, keep = coefficients
    fields, _, lanes = source.shape
    window = pl.ds(pl.multiple_of((tile - 1) * TILE, TILE), 3 * TILE)
    along_pitch, along_span, around, centre = [], [], [], []
    for g in range(fields):
        rows = source.at[g, window]
        here = rows[TILE : 2 * TILE, :]
        below = rows[TILE + 1 : 2 * TILE + 1, :][:, :width]
        above = rows[TILE - 1 : 2 * TILE - 1, :][:, :width]
        right = pltpu.roll(here, lanes - 1, 1)[:, :width]
        left = pltpu.roll(here, 1, 1)[:, :width]
        along_pitch.append(below - above)
        along_span.append(right - left)
        around.append((below + above) + (right + left))
        centre.append(here[:, :width])
    results = []
    for f in range(fields):
        total = keep[f] * centre[f] + near[f] * around[f]
        for g in range(fields):
            total = total + pitch[f][g] * along_pitch[g]
            total = total + span[f][g] * along_span[g]
        results.append(total)
    return results


def propagate_kernel(
    transposed, sign, scale, position, mat_pitch, mat_span, viscous, cells, extra, strip, upper, lower, lead, last, first, second
):
    fields, rows, cols = cells.shape
    lanes = cols + LANES
    has_left = position[0] > 0
    has_right = position[0] < position[1] - 1
    factor = sign * TIME_STEP * 0.5

    def entry(matrix, f, g):
        return factor * (matrix[g, f] if transposed else matrix[f, g])

    pitch = [[entry(mat_pitch, f, g) for g in range(fields)] for f in range(fields)]
    span = [[entry(mat_span, f, g) for g in range(fields)] for f in range(fields)]
    near = [TIME_STEP * viscous[f] for f in range(fields)]
    keep = [1.0 - 4.0 * TIME_STEP * viscous[f] for f in range(fields)]
    coefficients = (pitch, span, near, keep)

    def within(shape):
        side = lax.broadcasted_iota(jnp.int32, shape, 1) < LANES // 2
        return jnp.where(side, has_right.astype(jnp.int32), has_left.astype(jnp.int32)) > 0

    corner_above = jnp.concatenate([upper[f, :, cols:] for f in range(STRIP // TILE)], axis=0)
    corner_below = jnp.concatenate([lower[f, :, cols:] for f in range(STRIP // TILE)], axis=0)
    along = jnp.concatenate([corner_above, strip[...], corner_below], axis=1)
    along = jnp.concatenate([along, jnp.zeros((LANES - STRIP, along.shape[1]), jnp.float32)], axis=0)
    turned = jnp.transpose(along)[LANES - MARGIN : LANES + rows + MARGIN]
    inside = within(turned.shape)
    for f in range(fields):
        side = pltpu.roll(turned, LANES - (4 * f + 2), 1)
        first[f, :, cols:] = jnp.where(inside, side, 0.0)
        first[f, MARGIN - TILE : MARGIN, :cols] = upper[f, :, :cols]
        first[f, MARGIN + rows : MARGIN + rows + TILE, :cols] = lower[f, :, :cols]
        first[f, MARGIN : MARGIN + rows, :cols] = cells[f]

    inside_tile = within((TILE, LANES))

    def step_one(tile, carry):
        for f, value in enumerate(substep(first, tile, coefficients, lanes)):
            second[f, pl.ds(pl.multiple_of(tile * TILE, TILE), TILE), :cols] = value[:, :cols]
            second[f, pl.ds(pl.multiple_of(tile * TILE, TILE), TILE), cols:] = jnp.where(inside_tile, value[:, cols:], 0.0)
        return carry

    lax.fori_loop(1, (MARGIN + rows) // TILE + 1, step_one, 0, unroll=17)

    def step_two(result, base, tile, carry):
        for f, value in enumerate(substep(second, tile, coefficients, cols)):
            at = pl.multiple_of(tile * TILE - MARGIN, TILE)
            into = pl.multiple_of(at - base, TILE)
            result[f, pl.ds(into, TILE), :] = value + scale * extra[f, pl.ds(at, TILE), :]
        return carry

    begin = lead.shape[1]
    bounds = [MARGIN // TILE, (MARGIN + begin) // TILE, (MARGIN + rows) // TILE]
    lax.fori_loop(bounds[0], bounds[1], functools.partial(step_two, lead, 0), 0, unroll=7)
    lax.fori_loop(bounds[1], bounds[2], functools.partial(step_two, last, begin), 0, unroll=4)


def lead_kernel(adjoint, arrived, gradient):
    gradient[0] = adjoint[...] - arrived[...]


def last_kernel(adjoint, early, late, begun, gradient):
    gradient[0] = adjoint[...] - (early[...] + late[...])


def in_vmem(count):
    return [pl.BlockSpec(memory_space=pltpu.VMEM)] * count


def in_smem(count):
    return [pl.BlockSpec(memory_space=pltpu.SMEM)] * count


PARAMS = pltpu.CompilerParams(vmem_limit_bytes=VMEM_LIMIT)


def edges_of(cells):
    return pl.pallas_call(
        edges_kernel,
        out_shape=jax.ShapeDtypeStruct((STRIP, cells.shape[1]), jnp.float32),
        in_specs=in_vmem(1),
        out_specs=pl.BlockSpec(memory_space=pltpu.VMEM),
        compiler_params=PARAMS,
    )(cells)


def mismatch_of(lead, last, following):
    whole = jax.ShapeDtypeStruct(following.shape, jnp.float32)
    return pl.pallas_call(
        mismatch_kernel,
        out_shape=(whole, whole, jax.ShapeDtypeStruct((STRIP, following.shape[1]), jnp.float32)),
        in_specs=in_vmem(3),
        out_specs=tuple(in_vmem(3)),
        compiler_params=PARAMS,
    )(lead, last, following)


def gradient_of(adjoint, arrived):
    fields, begin, cols = adjoint[0].shape
    rest = adjoint[1].shape[1]
    whole = jax.ShapeDtypeStruct((1, fields, begin + rest, cols), jnp.float32)
    begun = pl.pallas_call(
        lead_kernel,
        grid=(1,),
        out_shape=whole,
        in_specs=in_vmem(2),
        out_specs=pl.BlockSpec((1, fields, begin, cols), lambda i: (0, 0, 0, 0)),
        compiler_params=PARAMS,
    )(adjoint[0], arrived[0])
    return pl.pallas_call(
        last_kernel,
        grid=(1,),
        out_shape=whole,
        in_specs=in_vmem(3) + [pl.BlockSpec(memory_space=pl.ANY)],
        out_specs=pl.BlockSpec((1, fields, rest, cols), lambda f: (0, 0, begin // rest, 0)),
        input_output_aliases={3: 0},
        compiler_params=PARAMS,
    )(adjoint[1], *arrived[1], begun)


def exchanged(cells, strip):
    fields, rows, cols = cells.shape
    count = lax.axis_size("span")
    if count == 2:
        sides = lax.ppermute(strip, "span", [(0, 1), (1, 0)])
    else:
        from_left = lax.ppermute(strip, "span", [(i, i + 1) for i in range(count - 1)])
        from_right = lax.ppermute(strip, "span", [(i + 1, i) for i in range(count - 1)])
        kind = lax.broadcasted_iota(jnp.int32, strip.shape, 0) % 4
        sides = jnp.where(kind < 2, from_left, from_right)

    def outer(row, lane):
        ends = sides[:, lane : lane + LANES].reshape(STRIP // TILE, TILE, LANES)
        ends = jnp.pad(ends, ((0, fields - STRIP // TILE), (0, 0), (0, 0)))
        return jnp.concatenate([cells[:, row : row + TILE, :], ends], axis=2)

    ring = lax.axis_size("pitch")
    upper = lax.ppermute(outer(rows - TILE, rows - LANES), "pitch", [(i, (i + 1) % ring) for i in range(ring)])
    lower = lax.ppermute(outer(0, 0), "pitch", [((i + 1) % ring, i) for i in range(ring)])
    return sides, upper, lower


def propagated(position, mat_pitch, mat_span, viscous, cells, extra, halos, transposed, sign, scale):
    fields, rows, cols = cells.shape
    wide = pltpu.VMEM((fields, rows + 2 * MARGIN, cols + LANES), jnp.float32)
    return pl.pallas_call(
        functools.partial(propagate_kernel, transposed, sign, scale),
        out_shape=tuple(jax.ShapeDtypeStruct((fields, n, cols), jnp.float32) for n in (rows - LAST, LAST)),
        in_specs=in_smem(4) + in_vmem(5),
        out_specs=tuple(in_vmem(2)),
        scratch_shapes=[wide, wide],
        compiler_params=PARAMS,
    )(position, mat_pitch, mat_span, viscous, cells, extra, *halos)


def passed_along(shard, by):
    count = lax.axis_size("seg")
    return lax.ppermute(shard, "seg", [(i, (i + by) % count) for i in range(count)])


def passed_by_swap(shard, after):
    count, width = lax.axis_size("seg"), lax.axis_size("span")
    held = lax.ppermute(shard, "seg", [(i, (i + 2) % count if i % 2 else i) for i in range(count)])

    def swapped(cells, parity):
        pairs = [(i * width + k, (i ^ 1) * width + k) for i in range(count) for k in range(parity, width, 2)]
        return lax.ppermute(cells, ("seg", "span"), pairs)

    early = swapped(held, 0)
    late = swapped(lax.optimization_barrier((held, after))[0], 1)
    return early, late


def body(states, forcing, adv_pitch, adv_span, diffusion):
    start = states[0]
    position = jnp.stack([lax.axis_index("span"), lax.axis_size("span")]).astype(jnp.int32)
    following = passed_along(start, -1)
    halos = exchanged(start, edges_of(start))
    ending = propagated(position, adv_pitch, adv_span, diffusion, start, forcing[0], halos, False, -1.0, TIME_STEP)
    arrived = [passed_along(ending[0], 1)]
    mismatch, again, strip = mismatch_of(*ending, following)
    halos = exchanged(again, strip)
    adjoint = propagated(position, adv_pitch, adv_span, diffusion, again, start, halos, True, 1.0, 1.0)
    arrived.append(passed_by_swap(ending[1], adjoint[0]))
    return (mismatch[None], gradient_of(adjoint, arrived))


def solution(mesh):
    whole = P("seg", None, "pitch", "span")
    return jax.shard_map(
        body,
        mesh=mesh,
        in_specs=(whole, whole, P(), P(), P()),
        out_specs=(whole, whole),
        check_vma=False,
    )
```

```python
import functools

import jax
import jax.numpy as jnp
from jax import lax
from jax.experimental import pallas as pl
from jax.experimental.pallas import tpu as pltpu
from jax.sharding import PartitionSpec as P

TIME_STEP = 0.25
SUBSTEPS = 2
TILE = 8
LANES = 128
STRIP = 24
MARGIN = 2 * TILE
LAST = 40
VMEM_LIMIT = 32 * 1024 * 1024


def edge_strip(field_of, fields, rows, cols):
    lane = lax.broadcasted_iota(jnp.int32, (rows, LANES), 1)
    packed = jnp.zeros((rows, LANES), jnp.float32)
    for f in range(fields):
        first, last = field_of(f, 0), field_of(f, cols - LANES)
        ends = jnp.where(lane < LANES // 2, first, last)
        moved = pltpu.roll(ends, 4 * f + 2, 1)
        packed = jnp.where((lane >= 4 * f) & (lane < 4 * f + 4), moved, packed)
    return jnp.transpose(packed)[:STRIP]


def edges_kernel(cells, strip):
    fields, rows, cols = cells.shape
    strip[...] = edge_strip(lambda f, at: cells[f, :, at : at + LANES], fields, rows, cols)


def mismatch_kernel(lead, last, following, mismatch, again, strip):
    fields, rows, cols = mismatch.shape
    begin = lead.shape[1]
    for f in range(fields):
        mismatch[f, :begin] = again[f, :begin] = lead[f] - following[f, :begin]
        mismatch[f, begin:] = again[f, begin:] = last[f] - following[f, begin:]
    strip[...] = edge_strip(lambda f, at: mismatch[f, :, at : at + LANES], fields, rows, cols)


def substep(source, tile, coefficients, width):
    pitch, span, near, keep = coefficients
    fields, _, lanes = source.shape
    window = pl.ds(pl.multiple_of((tile - 1) * TILE, TILE), 3 * TILE)
    along_pitch, along_span, around, centre = [], [], [], []
    for g in range(fields):
        rows = source.at[g, window]
        here = rows[TILE : 2 * TILE, :]
        below = rows[TILE + 1 : 2 * TILE + 1, :][:, :width]
        above = rows[TILE - 1 : 2 * TILE - 1, :][:, :width]
        right = pltpu.roll(here, lanes - 1, 1)[:, :width]
        left = pltpu.roll(here, 1, 1)[:, :width]
        along_pitch.append(below - above)
        along_span.append(right - left)
        around.append((below + above) + (right + left))
        centre.append(here[:, :width])
    results = []
    for f in range(fields):
        total = keep[f] * centre[f] + near[f] * around[f]
        for g in range(fields):
            total = total + pitch[f][g] * along_pitch[g]
            total = total + span[f][g] * along_span[g]
        results.append(total)
    return results


def propagate_kernel(
    transposed, sign, scale, position, mat_pitch, mat_span, viscous, cells, extra, strip, upper, lower, lead, last, first, second
):
    fields, rows, cols = cells.shape
    lanes = cols + LANES
    has_left = position[0] > 0
    has_right = position[0] < position[1] - 1
    factor = sign * TIME_STEP * 0.5

    def entry(matrix, f, g):
        return factor * (matrix[g, f] if transposed else matrix[f, g])

    pitch = [[entry(mat_pitch, f, g) for g in range(fields)] for f in range(fields)]
    span = [[entry(mat_span, f, g) for g in range(fields)] for f in range(fields)]
    near = [TIME_STEP * viscous[f] for f in range(fields)]
    keep = [1.0 - 4.0 * TIME_STEP * viscous[f] for f in range(fields)]
    coefficients = (pitch, span, near, keep)

    def within(shape):
        side = lax.broadcasted_iota(jnp.int32, shape, 1) < LANES // 2
        return jnp.where(side, has_right.astype(jnp.int32), has_left.astype(jnp.int32)) > 0

    corner_above = jnp.concatenate([upper[f, :, cols:] for f in range(STRIP // TILE)], axis=0)
    corner_below = jnp.concatenate([lower[f, :, cols:] for f in range(STRIP // TILE)], axis=0)
    along = jnp.concatenate([corner_above, strip[...], corner_below], axis=1)
    along = jnp.concatenate([along, jnp.zeros((LANES - STRIP, along.shape[1]), jnp.float32)], axis=0)
    turned = jnp.transpose(along)[LANES - MARGIN : LANES + rows + MARGIN]
    inside = within(turned.shape)
    for f in range(fields):
        side = pltpu.roll(turned, LANES - (4 * f + 2), 1)
        first[f, :, cols:] = jnp.where(inside, side, 0.0)
        first[f, MARGIN - TILE : MARGIN, :cols] = upper[f, :, :cols]
        first[f, MARGIN + rows : MARGIN + rows + TILE, :cols] = lower[f, :, :cols]
        first[f, MARGIN : MARGIN + rows, :cols] = cells[f]

    inside_tile = within((TILE, LANES))

    def step_one(tile, carry):
        for f, value in enumerate(substep(first, tile, coefficients, lanes)):
            second[f, pl.ds(pl.multiple_of(tile * TILE, TILE), TILE), :cols] = value[:, :cols]
            second[f, pl.ds(pl.multiple_of(tile * TILE, TILE), TILE), cols:] = jnp.where(inside_tile, value[:, cols:], 0.0)
        return carry

    lax.fori_loop(1, (MARGIN + rows) // TILE + 1, step_one, 0, unroll=17)

    def step_two(result, base, tile, carry):
        for f, value in enumerate(substep(second, tile, coefficients, cols)):
            at = pl.multiple_of(tile * TILE - MARGIN, TILE)
            into = pl.multiple_of(at - base, TILE)
            result[f, pl.ds(into, TILE), :] = value + scale * extra[f, pl.ds(at, TILE), :]
        return carry

    begin = lead.shape[1]
    bounds = [MARGIN // TILE, (MARGIN + begin) // TILE, (MARGIN + rows) // TILE]
    lax.fori_loop(bounds[0], bounds[1], functools.partial(step_two, lead, 0), 0, unroll=9)
    lax.fori_loop(bounds[1], bounds[2], functools.partial(step_two, last, begin), 0, unroll=last.shape[1] // TILE)


def lead_kernel(adjoint, arrived, gradient):
    gradient[0] = adjoint[...] - arrived[...]


def last_kernel(adjoint, early, late, begun, gradient, staged, done):
    staged[...] = adjoint[...] - (early[...] + late[...])
    rows = staged.shape[1]
    copy = pltpu.make_async_copy(staged, gradient.at[0, :, pl.ds(gradient.shape[2] - rows, rows)], done)
    copy.start()
    copy.wait()


def in_vmem(count):
    return [pl.BlockSpec(memory_space=pltpu.VMEM)] * count


def in_smem(count):
    return [pl.BlockSpec(memory_space=pltpu.SMEM)] * count


PARAMS = pltpu.CompilerParams(vmem_limit_bytes=VMEM_LIMIT)


def edges_of(cells):
    return pl.pallas_call(
        edges_kernel,
        out_shape=jax.ShapeDtypeStruct((STRIP, cells.shape[1]), jnp.float32),
        in_specs=in_vmem(1),
        out_specs=pl.BlockSpec(memory_space=pltpu.VMEM),
        compiler_params=PARAMS,
    )(cells)


def mismatch_of(lead, last, following):
    whole = jax.ShapeDtypeStruct(following.shape, jnp.float32)
    return pl.pallas_call(
        mismatch_kernel,
        out_shape=(whole, whole, jax.ShapeDtypeStruct((STRIP, following.shape[1]), jnp.float32)),
        in_specs=in_vmem(3),
        out_specs=tuple(in_vmem(3)),
        compiler_params=PARAMS,
    )(lead, last, following)


def gradient_of(adjoint, arrived):
    fields, begin, cols = adjoint[0].shape
    rest = adjoint[1].shape[1]
    whole = jax.ShapeDtypeStruct((1, fields, begin + rest, cols), jnp.float32)
    begun = pl.pallas_call(
        lead_kernel,
        grid=(1,),
        out_shape=whole,
        in_specs=in_vmem(2),
        out_specs=pl.BlockSpec((1, fields, begin, cols), lambda i: (0, 0, 0, 0)),
        compiler_params=PARAMS,
    )(adjoint[0], arrived[0])
    return pl.pallas_call(
        last_kernel,
        out_shape=whole,
        in_specs=in_vmem(3) + [pl.BlockSpec(memory_space=pl.ANY)],
        out_specs=pl.BlockSpec(memory_space=pl.ANY),
        scratch_shapes=[pltpu.VMEM((fields, rest, cols), jnp.float32), pltpu.SemaphoreType.DMA],
        input_output_aliases={3: 0},
        compiler_params=PARAMS,
    )(adjoint[1], *arrived[1], begun)


def exchanged(cells, strip):
    fields, rows, cols = cells.shape
    count = lax.axis_size("span")
    if count == 2:
        sides = lax.ppermute(strip, "span", [(0, 1), (1, 0)])
    else:
        from_left = lax.ppermute(strip, "span", [(i, i + 1) for i in range(count - 1)])
        from_right = lax.ppermute(strip, "span", [(i + 1, i) for i in range(count - 1)])
        kind = lax.broadcasted_iota(jnp.int32, strip.shape, 0) % 4
        sides = jnp.where(kind < 2, from_left, from_right)

    def outer(row, lane):
        ends = sides[:, lane : lane + LANES].reshape(STRIP // TILE, TILE, LANES)
        ends = jnp.pad(ends, ((0, fields - STRIP // TILE), (0, 0), (0, 0)))
        return jnp.concatenate([cells[:, row : row + TILE, :], ends], axis=2)

    ring = lax.axis_size("pitch")
    upper = lax.ppermute(outer(rows - TILE, rows - LANES), "pitch", [(i, (i + 1) % ring) for i in range(ring)])
    lower = lax.ppermute(outer(0, 0), "pitch", [((i + 1) % ring, i) for i in range(ring)])
    return sides, upper, lower


def propagated(position, mat_pitch, mat_span, viscous, cells, extra, halos, transposed, sign, scale):
    fields, rows, cols = cells.shape
    wide = pltpu.VMEM((fields, rows + 2 * MARGIN, cols + LANES), jnp.float32)
    return pl.pallas_call(
        functools.partial(propagate_kernel, transposed, sign, scale),
        out_shape=tuple(jax.ShapeDtypeStruct((fields, n, cols), jnp.float32) for n in (rows - LAST, LAST)),
        in_specs=in_smem(4) + in_vmem(5),
        out_specs=tuple(in_vmem(2)),
        scratch_shapes=[wide, wide],
        compiler_params=PARAMS,
    )(position, mat_pitch, mat_span, viscous, cells, extra, *halos)


def passed_along(shard, by):
    count = lax.axis_size("seg")
    return lax.ppermute(shard, "seg", [(i, (i + by) % count) for i in range(count)])


def passed_by_swap(shard, after):
    count, width = lax.axis_size("seg"), lax.axis_size("span")
    held = lax.ppermute(shard, "seg", [(i, (i + 2) % count if i % 2 else i) for i in range(count)])

    def swapped(cells, parity):
        pairs = [(i * width + k, (i ^ 1) * width + k) for i in range(count) for k in range(parity, width, 2)]
        return lax.ppermute(cells, ("seg", "span"), pairs)

    early = swapped(held, 0)
    late = swapped(lax.optimization_barrier((held, after))[0], 1)
    return early, late


def body(states, forcing, adv_pitch, adv_span, diffusion):
    start = states[0]
    position = jnp.stack([lax.axis_index("span"), lax.axis_size("span")]).astype(jnp.int32)
    following = passed_along(start, -1)
    halos = exchanged(start, edges_of(start))
    ending = propagated(position, adv_pitch, adv_span, diffusion, start, forcing[0], halos, False, -1.0, TIME_STEP)
    arrived = [passed_along(ending[0], 1)]
    mismatch, again, strip = mismatch_of(*ending, following)
    halos = exchanged(again, strip)
    adjoint = propagated(position, adv_pitch, adv_span, diffusion, again, start, halos, True, 1.0, 1.0)
    arrived.append(passed_by_swap(ending[1], adjoint[0]))
    return (mismatch[None], gradient_of(adjoint, arrived))


def solution(mesh):
    whole = P("seg", None, "pitch", "span")
    return jax.shard_map(
        body,
        mesh=mesh,
        in_specs=(whole, whole, P(), P(), P()),
        out_specs=(whole, whole),
        check_vma=False,
    )
```

```python
import functools

import jax
import jax.numpy as jnp
from jax import lax
from jax.experimental import pallas as pl
from jax.experimental.pallas import tpu as pltpu
from jax.sharding import PartitionSpec as P

TIME_STEP = 0.25
SUBSTEPS = 2
TILE = 8
LANES = 128
STRIP = 24
MARGIN = 2 * TILE
LAST = 40
VMEM_LIMIT = 32 * 1024 * 1024


def edge_strip(field_of, fields, rows, cols):
    lane = lax.broadcasted_iota(jnp.int32, (rows, LANES), 1)
    packed = jnp.zeros((rows, LANES), jnp.float32)
    for f in range(fields):
        first, last = field_of(f, 0), field_of(f, cols - LANES)
        ends = jnp.where(lane < LANES // 2, first, last)
        moved = pltpu.roll(ends, 4 * f + 2, 1)
        packed = jnp.where((lane >= 4 * f) & (lane < 4 * f + 4), moved, packed)
    return jnp.transpose(packed)[:STRIP]


def edges_kernel(cells, strip):
    fields, rows, cols = cells.shape
    strip[...] = edge_strip(lambda f, at: cells[f, :, at : at + LANES], fields, rows, cols)


def mismatch_kernel(lead, last, following, mismatch, again, strip):
    fields, rows, cols = mismatch.shape
    begin = lead.shape[1]
    for f in range(fields):
        mismatch[f, :begin] = again[f, :begin] = lead[f] - following[f, :begin]
        mismatch[f, begin:] = again[f, begin:] = last[f] - following[f, begin:]
    strip[...] = edge_strip(lambda f, at: mismatch[f, :, at : at + LANES], fields, rows, cols)


def substep(source, tile, coefficients, width):
    pitch, span, near, keep = coefficients
    fields, _, lanes = source.shape
    window = pl.ds(pl.multiple_of((tile - 1) * TILE, TILE), 3 * TILE)
    along_pitch, along_span, around, centre = [], [], [], []
    for g in range(fields):
        rows = source.at[g, window]
        here = rows[TILE : 2 * TILE, :]
        below = rows[TILE + 1 : 2 * TILE + 1, :][:, :width]
        above = rows[TILE - 1 : 2 * TILE - 1, :][:, :width]
        right = pltpu.roll(here, lanes - 1, 1)[:, :width]
        left = pltpu.roll(here, 1, 1)[:, :width]
        along_pitch.append(below - above)
        along_span.append(right - left)
        around.append((below + above) + (right + left))
        centre.append(here[:, :width])
    results = []
    for f in range(fields):
        total = keep[f] * centre[f] + near[f] * around[f]
        for g in range(fields):
            total = total + pitch[f][g] * along_pitch[g]
            total = total + span[f][g] * along_span[g]
        results.append(total)
    return results


def propagate_kernel(
    transposed, sign, scale, position, mat_pitch, mat_span, viscous, cells, extra, strip, upper, lower, lead, last, first, second
):
    fields, rows, cols = cells.shape
    lanes = cols + LANES
    has_left = position[0] > 0
    has_right = position[0] < position[1] - 1
    factor = sign * TIME_STEP * 0.5

    def entry(matrix, f, g):
        return factor * (matrix[g, f] if transposed else matrix[f, g])

    pitch = [[entry(mat_pitch, f, g) for g in range(fields)] for f in range(fields)]
    span = [[entry(mat_span, f, g) for g in range(fields)] for f in range(fields)]
    near = [TIME_STEP * viscous[f] for f in range(fields)]
    keep = [1.0 - 4.0 * TIME_STEP * viscous[f] for f in range(fields)]
    coefficients = (pitch, span, near, keep)

    def within(shape):
        side = lax.broadcasted_iota(jnp.int32, shape, 1) < LANES // 2
        return jnp.where(side, has_right.astype(jnp.int32), has_left.astype(jnp.int32)) > 0

    corner_above = jnp.concatenate([upper[f, :, cols:] for f in range(STRIP // TILE)], axis=0)
    corner_below = jnp.concatenate([lower[f, :, cols:] for f in range(STRIP // TILE)], axis=0)
    along = jnp.concatenate([corner_above, strip[...], corner_below], axis=1)
    along = jnp.concatenate([along, jnp.zeros((LANES - STRIP, along.shape[1]), jnp.float32)], axis=0)
    turned = jnp.transpose(along)[LANES - MARGIN : LANES + rows + MARGIN]
    inside = within(turned.shape)
    for f in range(fields):
        side = pltpu.roll(turned, LANES - (4 * f + 2), 1)
        first[f, :, cols:] = jnp.where(inside, side, 0.0)
        first[f, MARGIN - TILE : MARGIN, :cols] = upper[f, :, :cols]
        first[f, MARGIN + rows : MARGIN + rows + TILE, :cols] = lower[f, :, :cols]
        first[f, MARGIN : MARGIN + rows, :cols] = cells[f]

    inside_tile = within((TILE, LANES))

    def step_one(tile, carry):
        for f, value in enumerate(substep(first, tile, coefficients, lanes)):
            second[f, pl.ds(pl.multiple_of(tile * TILE, TILE), TILE), :cols] = value[:, :cols]
            second[f, pl.ds(pl.multiple_of(tile * TILE, TILE), TILE), cols:] = jnp.where(inside_tile, value[:, cols:], 0.0)
        return carry

    lax.fori_loop(1, (MARGIN + rows) // TILE + 1, step_one, 0, unroll=2)

    def step_two(result, base, tile, carry):
        for f, value in enumerate(substep(second, tile, coefficients, cols)):
            at = pl.multiple_of(tile * TILE - MARGIN, TILE)
            into = pl.multiple_of(at - base, TILE)
            result[f, pl.ds(into, TILE), :] = value + scale * extra[f, pl.ds(at, TILE), :]
        return carry

    begin = lead.shape[1]
    bounds = [MARGIN // TILE, (MARGIN + begin) // TILE, (MARGIN + rows) // TILE]
    lax.fori_loop(bounds[0], bounds[1], functools.partial(step_two, lead, 0), 0, unroll=9)
    lax.fori_loop(bounds[1], bounds[2], functools.partial(step_two, last, begin), 0, unroll=last.shape[1] // TILE)


def lead_kernel(adjoint, arrived, gradient):
    gradient[0] = adjoint[...] - arrived[...]


def last_kernel(adjoint, early, late, begun, gradient, staged, done):
    staged[...] = adjoint[...] - (early[...] + late[...])
    rows = staged.shape[1]
    copy = pltpu.make_async_copy(staged, gradient.at[0, :, pl.ds(gradient.shape[2] - rows, rows)], done)
    copy.start()
    copy.wait()


def in_vmem(count):
    return [pl.BlockSpec(memory_space=pltpu.VMEM)] * count


def in_smem(count):
    return [pl.BlockSpec(memory_space=pltpu.SMEM)] * count


PARAMS = pltpu.CompilerParams(vmem_limit_bytes=VMEM_LIMIT)


def edges_of(cells):
    return pl.pallas_call(
        edges_kernel,
        out_shape=jax.ShapeDtypeStruct((STRIP, cells.shape[1]), jnp.float32),
        in_specs=in_vmem(1),
        out_specs=pl.BlockSpec(memory_space=pltpu.VMEM),
        compiler_params=PARAMS,
    )(cells)


def mismatch_of(lead, last, following):
    whole = jax.ShapeDtypeStruct(following.shape, jnp.float32)
    return pl.pallas_call(
        mismatch_kernel,
        out_shape=(whole, whole, jax.ShapeDtypeStruct((STRIP, following.shape[1]), jnp.float32)),
        in_specs=in_vmem(3),
        out_specs=tuple(in_vmem(3)),
        compiler_params=PARAMS,
    )(lead, last, following)


def gradient_of(adjoint, arrived):
    fields, begin, cols = adjoint[0].shape
    rest = adjoint[1].shape[1]
    whole = jax.ShapeDtypeStruct((1, fields, begin + rest, cols), jnp.float32)
    begun = pl.pallas_call(
        lead_kernel,
        grid=(1,),
        out_shape=whole,
        in_specs=in_vmem(2),
        out_specs=pl.BlockSpec((1, fields, begin, cols), lambda i: (0, 0, 0, 0)),
        compiler_params=PARAMS,
    )(adjoint[0], arrived[0])
    return pl.pallas_call(
        last_kernel,
        out_shape=whole,
        in_specs=in_vmem(3) + [pl.BlockSpec(memory_space=pl.ANY)],
        out_specs=pl.BlockSpec(memory_space=pl.ANY),
        scratch_shapes=[pltpu.VMEM((fields, rest, cols), jnp.float32), pltpu.SemaphoreType.DMA],
        input_output_aliases={3: 0},
        compiler_params=PARAMS,
    )(adjoint[1], *arrived[1], begun)


def exchanged(cells, strip):
    fields, rows, cols = cells.shape
    count = lax.axis_size("span")
    if count == 2:
        sides = lax.ppermute(strip, "span", [(0, 1), (1, 0)])
    else:
        from_left = lax.ppermute(strip, "span", [(i, i + 1) for i in range(count - 1)])
        from_right = lax.ppermute(strip, "span", [(i + 1, i) for i in range(count - 1)])
        kind = lax.broadcasted_iota(jnp.int32, strip.shape, 0) % 4
        sides = jnp.where(kind < 2, from_left, from_right)

    def outer(row, lane):
        ends = sides[:, lane : lane + LANES].reshape(STRIP // TILE, TILE, LANES)
        ends = jnp.pad(ends, ((0, fields - STRIP // TILE), (0, 0), (0, 0)))
        return jnp.concatenate([cells[:, row : row + TILE, :], ends], axis=2)

    ring = lax.axis_size("pitch")
    upper = lax.ppermute(outer(rows - TILE, rows - LANES), "pitch", [(i, (i + 1) % ring) for i in range(ring)])
    lower = lax.ppermute(outer(0, 0), "pitch", [((i + 1) % ring, i) for i in range(ring)])
    return sides, upper, lower


def propagated(position, mat_pitch, mat_span, viscous, cells, extra, halos, transposed, sign, scale):
    fields, rows, cols = cells.shape
    wide = pltpu.VMEM((fields, rows + 2 * MARGIN, cols + LANES), jnp.float32)
    return pl.pallas_call(
        functools.partial(propagate_kernel, transposed, sign, scale),
        out_shape=tuple(jax.ShapeDtypeStruct((fields, n, cols), jnp.float32) for n in (rows - LAST, LAST)),
        in_specs=in_smem(4) + in_vmem(5),
        out_specs=tuple(in_vmem(2)),
        scratch_shapes=[wide, wide],
        compiler_params=PARAMS,
    )(position, mat_pitch, mat_span, viscous, cells, extra, *halos)


def passed_along(shard, by):
    count = lax.axis_size("seg")
    return lax.ppermute(shard, "seg", [(i, (i + by) % count) for i in range(count)])


def passed_by_swap(shard, after):
    count, width = lax.axis_size("seg"), lax.axis_size("span")
    held = lax.ppermute(shard, "seg", [(i, (i + 2) % count if i % 2 else i) for i in range(count)])

    def swapped(cells, parity):
        pairs = [(i * width + k, (i ^ 1) * width + k) for i in range(count) for k in range(parity, width, 2)]
        return lax.ppermute(cells, ("seg", "span"), pairs)

    early = swapped(held, 0)
    late = swapped(lax.optimization_barrier((held, after))[0], 1)
    return early, late


def body(states, forcing, adv_pitch, adv_span, diffusion):
    start = states[0]
    position = jnp.stack([lax.axis_index("span"), lax.axis_size("span")]).astype(jnp.int32)
    following = passed_along(start, -1)
    halos = exchanged(start, edges_of(start))
    ending = propagated(position, adv_pitch, adv_span, diffusion, start, forcing[0], halos, False, -1.0, TIME_STEP)
    arrived = [passed_along(ending[0], 1)]
    mismatch, again, strip = mismatch_of(*ending, following)
    halos = exchanged(again, strip)
    adjoint = propagated(position, adv_pitch, adv_span, diffusion, again, start, halos, True, 1.0, 1.0)
    arrived.append(passed_by_swap(ending[1], adjoint[0]))
    return (mismatch[None], gradient_of(adjoint, arrived))


def solution(mesh):
    whole = P("seg", None, "pitch", "span")
    return jax.shard_map(
        body,
        mesh=mesh,
        in_specs=(whole, whole, P(), P(), P()),
        out_specs=(whole, whole),
        check_vma=False,
    )
```

```python
import functools

import jax
import jax.numpy as jnp
from jax import lax
from jax.experimental import pallas as pl
from jax.experimental.pallas import tpu as pltpu
from jax.sharding import PartitionSpec as P

TIME_STEP = 0.25
SUBSTEPS = 2
TILE = 8
LANES = 128
STRIP = 24
MARGIN = 2 * TILE
LAST = 48
VMEM_LIMIT = 32 * 1024 * 1024


def edge_strip(field_of, fields, rows, cols):
    lane = lax.broadcasted_iota(jnp.int32, (rows, LANES), 1)
    packed = jnp.zeros((rows, LANES), jnp.float32)
    for f in range(fields):
        first, last = field_of(f, 0), field_of(f, cols - LANES)
        ends = jnp.where(lane < LANES // 2, first, last)
        moved = pltpu.roll(ends, 4 * f + 2, 1)
        packed = jnp.where((lane >= 4 * f) & (lane < 4 * f + 4), moved, packed)
    return jnp.transpose(packed)[:STRIP]


def edges_kernel(cells, strip):
    fields, rows, cols = cells.shape
    strip[...] = edge_strip(lambda f, at: cells[f, :, at : at + LANES], fields, rows, cols)


def mismatch_kernel(lead, last, following, mismatch, again, strip):
    fields, rows, cols = mismatch.shape
    begin = lead.shape[1]
    for f in range(fields):
        mismatch[f, :begin] = again[f, :begin] = lead[f] - following[f, :begin]
        mismatch[f, begin:] = again[f, begin:] = last[f] - following[f, begin:]
    strip[...] = edge_strip(lambda f, at: mismatch[f, :, at : at + LANES], fields, rows, cols)


def substep(source, tile, coefficients, width):
    pitch, span, near, keep = coefficients
    fields, _, lanes = source.shape
    window = pl.ds(pl.multiple_of((tile - 1) * TILE, TILE), 3 * TILE)
    along_pitch, along_span, around, centre = [], [], [], []
    for g in range(fields):
        rows = source.at[g, window]
        here = rows[TILE : 2 * TILE, :]
        below = rows[TILE + 1 : 2 * TILE + 1, :][:, :width]
        above = rows[TILE - 1 : 2 * TILE - 1, :][:, :width]
        right = pltpu.roll(here, lanes - 1, 1)[:, :width]
        left = pltpu.roll(here, 1, 1)[:, :width]
        along_pitch.append(below - above)
        along_span.append(right - left)
        around.append((below + above) + (right + left))
        centre.append(here[:, :width])
    results = []
    for f in range(fields):
        total = keep[f] * centre[f] + near[f] * around[f]
        for g in range(fields):
            total = total + pitch[f][g] * along_pitch[g]
            total = total + span[f][g] * along_span[g]
        results.append(total)
    return results


def propagate_kernel(
    transposed, sign, scale, position, mat_pitch, mat_span, viscous, cells, extra, strip, upper, lower, lead, last, first, second
):
    fields, rows, cols = cells.shape
    lanes = cols + LANES
    has_left = position[0] > 0
    has_right = position[0] < position[1] - 1
    factor = sign * TIME_STEP * 0.5

    def entry(matrix, f, g):
        return factor * (matrix[g, f] if transposed else matrix[f, g])

    pitch = [[entry(mat_pitch, f, g) for g in range(fields)] for f in range(fields)]
    span = [[entry(mat_span, f, g) for g in range(fields)] for f in range(fields)]
    near = [TIME_STEP * viscous[f] for f in range(fields)]
    keep = [1.0 - 4.0 * TIME_STEP * viscous[f] for f in range(fields)]
    coefficients = (pitch, span, near, keep)

    def within(shape):
        side = lax.broadcasted_iota(jnp.int32, shape, 1) < LANES // 2
        return jnp.where(side, has_right.astype(jnp.int32), has_left.astype(jnp.int32)) > 0

    corner_above = jnp.concatenate([upper[f, :, cols:] for f in range(STRIP // TILE)], axis=0)
    corner_below = jnp.concatenate([lower[f, :, cols:] for f in range(STRIP // TILE)], axis=0)
    along = jnp.concatenate([corner_above, strip[...], corner_below], axis=1)
    along = jnp.concatenate([along, jnp.zeros((LANES - STRIP, along.shape[1]), jnp.float32)], axis=0)
    turned = jnp.transpose(along)[LANES - MARGIN : LANES + rows + MARGIN]
    inside = within(turned.shape)
    for f in range(fields):
        side = pltpu.roll(turned, LANES - (4 * f + 2), 1)
        first[f, :, cols:] = jnp.where(inside, side, 0.0)
        first[f, MARGIN - TILE : MARGIN, :cols] = upper[f, :, :cols]
        first[f, MARGIN + rows : MARGIN + rows + TILE, :cols] = lower[f, :, :cols]
        first[f, MARGIN : MARGIN + rows, :cols] = cells[f]

    inside_tile = within((TILE, LANES))

    def step_one(tile, carry):
        for f, value in enumerate(substep(first, tile, coefficients, lanes)):
            second[f, pl.ds(pl.multiple_of(tile * TILE, TILE), TILE), :cols] = value[:, :cols]
            second[f, pl.ds(pl.multiple_of(tile * TILE, TILE), TILE), cols:] = jnp.where(inside_tile, value[:, cols:], 0.0)
        return carry

    lax.fori_loop(1, (MARGIN + rows) // TILE + 1, step_one, 0, unroll=17)

    def step_two(result, base, tile, carry):
        for f, value in enumerate(substep(second, tile, coefficients, cols)):
            at = pl.multiple_of(tile * TILE - MARGIN, TILE)
            into = pl.multiple_of(at - base, TILE)
            result[f, pl.ds(into, TILE), :] = value + scale * extra[f, pl.ds(at, TILE), :]
        return carry

    begin = lead.shape[1]
    bounds = [MARGIN // TILE, (MARGIN + begin) // TILE, (MARGIN + rows) // TILE]
    lax.fori_loop(bounds[0], bounds[1], functools.partial(step_two, lead, 0), 0, unroll=2)
    lax.fori_loop(bounds[1], bounds[2], functools.partial(step_two, last, begin), 0, unroll=last.shape[1] // TILE)


def lead_kernel(adjoint, arrived, gradient):
    gradient[0] = adjoint[...] - arrived[...]


def last_kernel(adjoint, early, late, begun, gradient, staged, done):
    staged[...] = adjoint[...] - (early[...] + late[...])
    rows = staged.shape[1]
    copy = pltpu.make_async_copy(staged, gradient.at[0, :, pl.ds(gradient.shape[2] - rows, rows)], done)
    copy.start()
    copy.wait()


def in_vmem(count):
    return [pl.BlockSpec(memory_space=pltpu.VMEM)] * count


def in_smem(count):
    return [pl.BlockSpec(memory_space=pltpu.SMEM)] * count


PARAMS = pltpu.CompilerParams(vmem_limit_bytes=VMEM_LIMIT)


def edges_of(cells):
    return pl.pallas_call(
        edges_kernel,
        out_shape=jax.ShapeDtypeStruct((STRIP, cells.shape[1]), jnp.float32),
        in_specs=in_vmem(1),
        out_specs=pl.BlockSpec(memory_space=pltpu.VMEM),
        compiler_params=PARAMS,
    )(cells)


def mismatch_of(lead, last, following):
    whole = jax.ShapeDtypeStruct(following.shape, jnp.float32)
    return pl.pallas_call(
        mismatch_kernel,
        out_shape=(whole, whole, jax.ShapeDtypeStruct((STRIP, following.shape[1]), jnp.float32)),
        in_specs=in_vmem(3),
        out_specs=tuple(in_vmem(3)),
        compiler_params=PARAMS,
    )(lead, last, following)


def gradient_of(adjoint, arrived):
    fields, begin, cols = adjoint[0].shape
    rest = adjoint[1].shape[1]
    whole = jax.ShapeDtypeStruct((1, fields, begin + rest, cols), jnp.float32)
    begun = pl.pallas_call(
        lead_kernel,
        grid=(1,),
        out_shape=whole,
        in_specs=in_vmem(2),
        out_specs=pl.BlockSpec((1, fields, begin, cols), lambda i: (0, 0, 0, 0)),
        compiler_params=PARAMS,
    )(adjoint[0], arrived[0])
    return pl.pallas_call(
        last_kernel,
        out_shape=whole,
        in_specs=in_vmem(3) + [pl.BlockSpec(memory_space=pl.ANY)],
        out_specs=pl.BlockSpec(memory_space=pl.ANY),
        scratch_shapes=[pltpu.VMEM((fields, rest, cols), jnp.float32), pltpu.SemaphoreType.DMA],
        input_output_aliases={3: 0},
        compiler_params=PARAMS,
    )(adjoint[1], *arrived[1], begun)


def exchanged(cells, strip):
    fields, rows, cols = cells.shape
    count = lax.axis_size("span")
    if count == 2:
        sides = lax.ppermute(strip, "span", [(0, 1), (1, 0)])
    else:
        from_left = lax.ppermute(strip, "span", [(i, i + 1) for i in range(count - 1)])
        from_right = lax.ppermute(strip, "span", [(i + 1, i) for i in range(count - 1)])
        kind = lax.broadcasted_iota(jnp.int32, strip.shape, 0) % 4
        sides = jnp.where(kind < 2, from_left, from_right)

    def outer(row, lane):
        ends = sides[:, lane : lane + LANES].reshape(STRIP // TILE, TILE, LANES)
        ends = jnp.pad(ends, ((0, fields - STRIP // TILE), (0, 0), (0, 0)))
        return jnp.concatenate([cells[:, row : row + TILE, :], ends], axis=2)

    ring = lax.axis_size("pitch")
    upper = lax.ppermute(outer(rows - TILE, rows - LANES), "pitch", [(i, (i + 1) % ring) for i in range(ring)])
    lower = lax.ppermute(outer(0, 0), "pitch", [((i + 1) % ring, i) for i in range(ring)])
    return sides, upper, lower


def propagated(position, mat_pitch, mat_span, viscous, cells, extra, halos, transposed, sign, scale):
    fields, rows, cols = cells.shape
    wide = pltpu.VMEM((fields, rows + 2 * MARGIN, cols + LANES), jnp.float32)
    return pl.pallas_call(
        functools.partial(propagate_kernel, transposed, sign, scale),
        out_shape=tuple(jax.ShapeDtypeStruct((fields, n, cols), jnp.float32) for n in (rows - LAST, LAST)),
        in_specs=in_smem(4) + in_vmem(5),
        out_specs=tuple(in_vmem(2)),
        scratch_shapes=[wide, wide],
        compiler_params=PARAMS,
    )(position, mat_pitch, mat_span, viscous, cells, extra, *halos)


def passed_along(shard, by):
    count = lax.axis_size("seg")
    return lax.ppermute(shard, "seg", [(i, (i + by) % count) for i in range(count)])


def passed_by_swap(shard, after):
    count, width = lax.axis_size("seg"), lax.axis_size("span")
    held = lax.ppermute(shard, "seg", [(i, (i + 2) % count if i % 2 else i) for i in range(count)])

    def swapped(cells, parity):
        pairs = [(i * width + k, (i ^ 1) * width + k) for i in range(count) for k in range(parity, width, 2)]
        return lax.ppermute(cells, ("seg", "span"), pairs)

    early = swapped(held, 0)
    late = swapped(lax.optimization_barrier((held, after))[0], 1)
    return early, late


def body(states, forcing, adv_pitch, adv_span, diffusion):
    start = states[0]
    position = jnp.stack([lax.axis_index("span"), lax.axis_size("span")]).astype(jnp.int32)
    following = passed_along(start, -1)
    halos = exchanged(start, edges_of(start))
    ending = propagated(position, adv_pitch, adv_span, diffusion, start, forcing[0], halos, False, -1.0, TIME_STEP)
    arrived = [passed_along(ending[0], 1)]
    mismatch, again, strip = mismatch_of(*ending, following)
    halos = exchanged(again, strip)
    adjoint = propagated(position, adv_pitch, adv_span, diffusion, again, start, halos, True, 1.0, 1.0)
    arrived.append(passed_by_swap(ending[1], adjoint[0]))
    return (mismatch[None], gradient_of(adjoint, arrived))


def solution(mesh):
    whole = P("seg", None, "pitch", "span")
    return jax.shard_map(
        body,
        mesh=mesh,
        in_specs=(whole, whole, P(), P(), P()),
        out_specs=(whole, whole),
        check_vma=False,
    )
```
